128 devices in a mesh: ctxa: 16 (over y_hi, x, core), ctxb: 8 (over y_lo, z).
Axes of the slice: x: 4, y: 4 (y_hi: 2, y_lo: 2; y = y_hi * 2 + y_lo), z: 4, core: 2. Of those that a mesh axis runs over, the one named last changes fastest.
Arguments:
- queries: bfloat16 [16384, 768], P(('ctxa', 'ctxb')), may hold values from -64 to 64
- keys: bfloat16 [16384, 128], P(('ctxa', 'ctxb')), may hold values from -6 to 6
- values: bfloat16 [16384, 128], P(('ctxa', 'ctxb')), may hold values from -6 to 6
- grad_out: bfloat16 [16384, 768], P(('ctxa', 'ctxb')), may hold values from -6 to 6
Outputs:
- attended: bfloat16 [16384, 768], P(('ctxa', 'ctxb'))
- grad_q: bfloat16 [16384, 768], P(('ctxa', 'ctxb'))
- grad_k: bfloat16 [16384, 128], P(('ctxa', 'ctxb'))
- grad_v: bfloat16 [16384, 128], P(('ctxa', 'ctxb'))
The draws below stay inside these ranges and needn't reach their ends.
All inputs are finite; a program needn't handle non-finite values.
Results may differ from the reference program's by a relative error of at most 0.035.
Values may be sent and summed in bfloat16 or wider, within the bound.
A program may use at most 128 MiB of HBM per device.

```python
import jax
import jax.numpy as jnp
from jax import lax

HEADS = 6
HEAD_DIM = 128
SEQ = 16384


def draw_keys(key, part):
    key = jax.random.fold_in(key, 7)
    drawn = jax.random.truncated_normal(key, -6.0, 6.0, (SEQ, HEAD_DIM), jnp.float32)
    return drawn.astype(jnp.bfloat16)


def draw_queries(key, part):
    key = jax.random.fold_in(key, 9)
    drawn = jax.random.truncated_normal(key, -6.0, 6.0, (SEQ, HEADS * HEAD_DIM), jnp.float32)
    return drawn.astype(jnp.bfloat16)


def block_levels(own_key, dims, shards, smallest, largest):
    loudness = 1.0
    for dim, blocks in shards:
        draws = jax.random.uniform(jax.random.fold_in(jax.random.fold_in(own_key, 6), dim), (blocks,), jnp.float32, smallest / len(shards), largest / len(shards))
        loudness = loudness * jnp.repeat(jnp.exp(draws), dims[dim] // blocks).reshape((-1,) + (1,) * (len(dims) - 1 - dim))
    return loudness


def bell_draw(key, dims, deviation, reach, pieces=(), kind=jnp.bfloat16):
    entries = jax.random.normal(key, dims, jnp.float32) * deviation
    if len(pieces) > 0:
        entries = block_levels(key, dims, pieces, -0.22, 0.18) * entries
    return jnp.clip(entries, min=-reach, max=reach).astype(kind)


def setup_inputs(seed: int = 0) -> dict:
    splits = jax.random.split(jax.random.key(seed), 5)
    return {
        "queries": draw_queries(jax.random.fold_in(splits[4], 71), 0),
        "keys": draw_keys(jax.random.fold_in(splits[4], 71), 0),
        "values": bell_draw(splits[2], (SEQ, HEAD_DIM), 1.0, 6.0, ((0, 128),)),
        "grad_out": bell_draw(splits[3], (SEQ, HEADS * HEAD_DIM), 1.0, 6.0, ((0, 128),)),
    }


MASKED = -1e30


def reference(queries, keys, values, grad_out):
    seq_len = queries.shape[0]
    score_scale = HEAD_DIM ** -0.5
    block_len = 256 if seq_len % 256 == 0 else seq_len
    block_count = seq_len // block_len
    query_heads = queries.reshape(seq_len, HEADS, HEAD_DIM)
    grad_heads = grad_out.reshape(seq_len, HEADS, HEAD_DIM)
    key_f = keys.astype(jnp.float32)
    value_f = values.astype(jnp.float32)
    key_pos = jnp.arange(seq_len, dtype=jnp.int32)

    def prepare(block_id):
        first_row = (block_id * block_len).astype(jnp.int32)
        query_f = lax.dynamic_slice_in_dim(query_heads, first_row, block_len, 0).astype(jnp.float32)
        query_pos = first_row + jnp.arange(block_len, dtype=jnp.int32)
        visible = key_pos[None, :] <= query_pos[:, None]
        scores = jnp.where(visible[None], jnp.einsum("qhd,kd->hqk", query_f, key_f) * score_scale, MASKED)
        return first_row, query_f, visible, scores

    def forward(block_id):
        first_row, query_f, visible, scores = prepare(block_id)
        row_max = jnp.max(scores, axis=-1)
        row_sum = jnp.sum(jnp.where(visible[None], jnp.exp(scores - row_max[..., None]), 0.0), axis=-1)
        log_total = row_max + jnp.log(row_sum)
        probs = jnp.where(visible[None], jnp.exp(scores - log_total[..., None]), 0.0)
        weights = lax.optimization_barrier(probs.astype(jnp.bfloat16)).astype(jnp.float32)
        attended = jnp.einsum("hqk,kd->qhd", weights, value_f).astype(jnp.bfloat16)
        return attended, log_total

    outputs, log_totals = lax.map(forward, jnp.arange(block_count, dtype=jnp.int32))
    attended = outputs.reshape(seq_len, HEADS * HEAD_DIM)

    def backward(carried, block_id):
        grad_key, grad_value = carried
        first_row, query_f, visible, scores = prepare(block_id)
        log_total = log_totals[block_id]
        out_f = outputs[block_id].astype(jnp.float32)
        grad_f = lax.dynamic_slice_in_dim(grad_heads, first_row, block_len, 0).astype(jnp.float32)
        delta = jnp.sum(grad_f * out_f, axis=-1).T
        probs = jnp.where(visible[None], jnp.exp(scores - log_total[..., None]), 0.0)
        weights = lax.optimization_barrier(probs.astype(jnp.bfloat16)).astype(jnp.float32)
        dweights = jnp.einsum("qhd,kd->hqk", grad_f, value_f)
        dscores = lax.optimization_barrier((probs * (dweights - delta[..., None]) * score_scale).astype(jnp.bfloat16)).astype(jnp.float32)
        grad_query = jnp.einsum("hqk,kd->qhd", dscores, key_f).astype(jnp.bfloat16)
        grad_key = grad_key + jnp.einsum("hqk,qhd->kd", dscores, query_f)
        grad_value = grad_value + jnp.einsum("hqk,qhd->kd", weights, grad_f)
        return (grad_key, grad_value), grad_query

    zeros_kv = jnp.zeros((seq_len, HEAD_DIM), jnp.float32)
    (grad_key, grad_value), grad_query = lax.scan(backward, (zeros_kv, zeros_kv), jnp.arange(block_count, dtype=jnp.int32))
    return attended, grad_query.reshape(seq_len, HEADS * HEAD_DIM), grad_key.astype(jnp.bfloat16), grad_value.astype(jnp.bfloat16)
```

```python
import functools
import math

import jax
import jax.numpy as jnp
from jax import lax
from jax.experimental import pallas as pl
from jax.experimental.pallas import tpu as pltpu
from jax.sharding import PartitionSpec as P

MESH = pl.DeviceIdType.MESH
BF16 = jnp.bfloat16
F32 = jnp.float32

HEADS = 6
D = 128
T = 128
QC = HEADS * T
NS = 32
NZ = 4
CB = 2
CK = CB * T
NCH = NS // CB
MAXP = 36
SCALE = D ** -0.5
C2 = SCALE * math.log2(math.e)
LOW = -1e30


def group_row(s, z, b):
    flip = (b + z) % 2
    return s + flip * (NS - 1 - 2 * s)


def chunks_of(s, z, b):
    seen = group_row(s, z, b) + (b >= z).astype(jnp.int32)
    return (seen + CB - 1) // CB


def base_of(s, z, b):
    total = jnp.int32(0)
    for other in range(NZ):
        total = total + jnp.where(other < b, chunks_of(s, z, jnp.int32(other)), 0)
    return total


def transpose_heads(qg, qgt, b):
    for which in range(2):
        for h in range(HEADS):
            rows = pl.ds(which * QC + h * T, T)
            qgt[b, pl.ds(which * D, D), pl.ds(h * T, T)] = qg[b, rows, :].T


def transpose_kv(kv, kvt, block):
    half = block % CB
    for lane in range(CB):

        @pl.when(half == lane)
        def _():
            for which in range(2):
                kvt[block // CB, pl.ds(which * D, D), pl.ds(lane * T, T)] = kv[
                    block, pl.ds(which * T, T), :
                ].T


def key_rows(kv, c):
    return kv[pl.ds(c * CB, CB), pl.ds(0, T), :].reshape(CK, D)


def value_rows(kv, c):
    return kv[pl.ds(c * CB, CB), pl.ds(T, T), :].reshape(CK, D)


def forward_block(s, z, b, kv, kvt, qgt, scores, probs, out_t, stats):
    count = chunks_of(s, z, b)
    base = base_of(s, z, b)
    q_block = group_row(s, z, b) * NZ + b

    def score(c):
        return jnp.dot(key_rows(kv, c), qgt[b, pl.ds(0, D), :], preferred_element_type=F32)

    def top(x):
        return jnp.max(x.reshape(CK // 8, 8, QC), axis=0)

    def score_step(c, high):
        x = score(c)
        scores[c] = x
        return jnp.maximum(high, top(x))

    def last_step(c, high):
        x = score(c)
        row = lax.broadcasted_iota(jnp.int32, (CK, QC), 0)
        col = lax.broadcasted_iota(jnp.int32, (CK, QC), 1)
        key_pos = ((c * CB + row // T) * NZ + z) * T + row % T
        q_pos = q_block * T + col % T
        x = jnp.where(key_pos <= q_pos, x, LOW)
        scores[c] = x
        return jnp.maximum(high, top(x))

    high = jnp.full((8, QC), LOW, F32)
    high = lax.fori_loop(0, count - 1, score_step, high)
    high = lax.fori_loop(jnp.maximum(count - 1, 0), count, last_step, high)
    row_max = jnp.max(high, axis=0, keepdims=True) * C2

    out_t[b] = jnp.zeros((D, QC), F32)

    def prob_step(c, total):
        p = jnp.exp2(scores[c] * C2 - row_max)
        total = total + jnp.sum(p.reshape(CK // 8, 8, QC), axis=0)
        pb = p.astype(BF16)
        probs[base + c] = pb
        out_t[b] += jnp.dot(kvt[c, pl.ds(D, D), :], pb, preferred_element_type=F32)
        return total

    total = lax.fori_loop(0, count, prob_step, jnp.zeros((8, QC), F32))
    row_sum = jnp.sum(total, axis=0, keepdims=True)
    part_delta = jnp.sum(qgt[b, pl.ds(D, D), :].astype(F32) * out_t[b], axis=0, keepdims=True)
    stats[b, z] = jnp.concatenate(
        [row_max, row_sum, part_delta, jnp.zeros((5, QC), F32)], axis=0
    )


def merge_stats(z, b, stats, coef, delta):
    highs = [stats[b, j, pl.ds(0, 1), :] for j in range(NZ)]
    high = functools.reduce(jnp.maximum, highs)
    facs = [jnp.exp2(x - high) for x in highs]
    total = sum(stats[b, j, pl.ds(1, 1), :] * facs[j] for j in range(NZ))
    inv = 1.0 / total
    coef[b] = jnp.exp2(stats[b, z, pl.ds(0, 1), :] - high) * inv
    delta[b] = sum(stats[b, j, pl.ds(2, 1), :] * facs[j] for j in range(NZ)) * inv
    return [f * inv for f in facs]


def backward_tile(s, z, b, c, kv, kvt, qg, qgt, probs, coef, delta, dq_t, dkv):
    base = base_of(s, z, b)
    dw = jnp.dot(value_rows(kv, c), qgt[b, pl.ds(D, D), :], preferred_element_type=F32)
    w = probs[base + c].astype(F32) * coef[b]
    ds = (w * (dw - delta[b])).astype(BF16)
    wb = w.astype(BF16)
    dkv[:, pl.ds(0, D)] += jnp.dot(ds, qg[b, pl.ds(0, QC), :], preferred_element_type=F32)
    dkv[:, pl.ds(D, D)] += jnp.dot(wb, qg[b, pl.ds(QC, QC), :], preferred_element_type=F32)
    dq_t[b] += jnp.dot(kvt[c, pl.ds(0, D), :], ds, preferred_element_type=F32)


def kernel(
    q_ref, k_ref, v_ref, g_ref,
    att_ref, gq_ref, gk_ref, gv_ref,
    kv, kvt, qg, qgt, scores, probs, out_t, dq_t, stats, coef, delta, dkv,
    kv_out, kv_in, o_out, o_in, dq_out, dq_in,
    kv_send, kv_recv, fwd_send, q_send, q_recv, st_send, st_recv,
    o_send, o_recv, dq_send, dq_recv, dkv_send, dkv_recv,
):
    ia = lax.axis_index("ctxa")
    ib = lax.axis_index("ctxb")
    z = ib % NZ
    s = ia * 2 + ib // NZ

    def device(row, plane):
        return (row // 2, (row % 2) * NZ + plane)

    core = ia % 2
    sibling = s + 2 - 4 * core

    def same_core(i):
        own = (s // 4) * 2 + s % 2
        j = (own + i) % (NS // 2)
        return (j // 2) * 4 + core * 2 + j % 2

    barrier = pltpu.get_barrier_semaphore()

    def greet(i, _):
        pl.semaphore_signal(
            barrier, inc=1, device_id=device((s + i) % NS, z), device_id_type=MESH
        )
        return 0

    lax.fori_loop(1, NS, greet, 0)
    for i in range(1, NZ):
        b = (z + i) % NZ
        pl.semaphore_signal(
            barrier, inc=1, device_id=device(group_row(s, z, b), b), device_id_type=MESH
        )

    kv[s, pl.ds(0, T), :] = k_ref[...]
    kv[s, pl.ds(T, T), :] = v_ref[...]
    for h in range(HEADS):
        qg[z, pl.ds(h * T, T), :] = q_ref[:, pl.ds(h * D, D)]
        qg[z, pl.ds(QC + h * T, T), :] = g_ref[:, pl.ds(h * D, D)]

    pl.semaphore_wait(barrier, NS - 1 + NZ - 1)

    def kv_copy(i):
        return pltpu.make_async_remote_copy(
            src_ref=kv.at[s],
            dst_ref=kv.at[s],
            send_sem=kv_send.at[i],
            recv_sem=kv_recv.at[s],
            device_id=device(same_core(i), z),
            device_id_type=MESH,
        )

    def start_kv(i, _):
        kv_copy(i).start()
        return 0

    lax.fori_loop(1, NS // 2, start_kv, 0)

    def q_copy(i):
        b = (z + i) % NZ
        return pltpu.make_async_remote_copy(
            src_ref=qg.at[z],
            dst_ref=qg.at[z],
            send_sem=q_send.at[i],
            recv_sem=q_recv.at[z],
            device_id=device(group_row(s, z, b), b),
            device_id_type=MESH,
        )

    def start_q(i, _):
        q_copy(i).start()
        return 0

    lax.fori_loop(1, NZ, start_q, 0)
    transpose_heads(qg, qgt, z)

    def wait_block(row):
        pltpu.make_async_remote_copy(
            src_ref=kv.at[row],
            dst_ref=kv.at[row],
            send_sem=kv_send.at[0],
            recv_sem=kv_recv.at[row],
            device_id=device(sibling, z),
            device_id_type=MESH,
        ).wait_recv()

    def pass_copy(i):
        row = same_core(i)
        return pltpu.make_async_remote_copy(
            src_ref=kv.at[row],
            dst_ref=kv.at[row],
            send_sem=fwd_send.at[i],
            recv_sem=kv_recv.at[row],
            device_id=device(sibling, z),
            device_id_type=MESH,
        )

    def pass_step(i, _):
        row = same_core(i)

        @pl.when(i > 0)
        def _():
            wait_block(row)

        pass_copy(i).start()
        transpose_kv(kv, kvt, row)
        return 0

    lax.fori_loop(0, NS // 2, pass_step, 0)

    def other_step(i, _):
        row = same_core(i)
        row = row + 2 - 4 * core
        wait_block(row)
        transpose_kv(kv, kvt, row)
        return 0

    lax.fori_loop(0, NS // 2, other_step, 0)

    def st_copy(b, i):
        p = (z + i) % NZ
        return pltpu.make_async_remote_copy(
            src_ref=stats.at[b, z],
            dst_ref=stats.at[b, z],
            send_sem=st_send.at[b, i],
            recv_sem=st_recv.at[b, z],
            device_id=device(group_row(s, z, p), p),
            device_id_type=MESH,
        )

    def o_copy(b):
        return pltpu.make_async_remote_copy(
            src_ref=o_out.at[b],
            dst_ref=o_in.at[z],
            send_sem=o_send.at[b],
            recv_sem=o_recv.at[z],
            device_id=device(group_row(s, z, b), b),
            device_id_type=MESH,
        )

    def dq_copy(b):
        return pltpu.make_async_remote_copy(
            src_ref=dq_out.at[b],
            dst_ref=dq_in.at[z],
            send_sem=dq_send.at[b],
            recv_sem=dq_recv.at[z],
            device_id=device(group_row(s, z, b), b),
            device_id_type=MESH,
        )

    def forward_step(i, _):
        b = (z + i) % NZ

        @pl.when(i > 0)
        def _():
            pltpu.make_async_remote_copy(
                src_ref=qg.at[b],
                dst_ref=qg.at[b],
                send_sem=q_send.at[0],
                recv_sem=q_recv.at[b],
                device_id=device(group_row(s, z, b), b),
                device_id_type=MESH,
            ).wait_recv()
            transpose_heads(qg, qgt, b)

        forward_block(s, z, b, kv, kvt, qgt, scores, probs, out_t, stats)
        lax.fori_loop(1, NZ, lambda j, _: (st_copy(b, j).start(), 0)[1], 0)

        @pl.when(i > 0)
        def _():
            o_out[b] = out_t[b].astype(BF16)
            o_copy(b).start()

        return 0

    lax.fori_loop(0, NZ, forward_step, 0)

    def wait_stats(b, p):
        pltpu.make_async_remote_copy(
            src_ref=stats.at[b, p],
            dst_ref=stats.at[b, p],
            send_sem=st_send.at[b, 0],
            recv_sem=st_recv.at[b, p],
            device_id=device(group_row(s, z, p), p),
            device_id_type=MESH,
        ).wait_recv()

    def merge_step(b, _):
        lax.fori_loop(1, NZ, lambda j, _: (wait_stats(b, (z + j) % NZ), 0)[1], 0)
        merge_stats(z, b, stats, coef, delta)
        dq_t[b] = jnp.zeros((D, QC), F32)
        return 0

    lax.fori_loop(0, NZ, merge_step, 0)

    def dkv_copy(row):
        return pltpu.make_async_remote_copy(
            src_ref=kv_out.at[row],
            dst_ref=kv_in.at[s],
            send_sem=dkv_send.at[row],
            recv_sem=dkv_recv.at[s],
            device_id=device(row, z),
            device_id_type=MESH,
        )

    def chunk_step(c, _):
        dkv[...] = jnp.zeros((CK, 2 * D), F32)

        def tile_step(b, _):
            count = chunks_of(s, z, b)

            @pl.when(c < count)
            def _():
                backward_tile(
                    s, z, b, c, kv, kvt, qg, qgt, probs, coef, delta, dq_t, dkv
                )

            @pl.when((c == jnp.maximum(count - 1, 0)) & (b != z))
            def _():
                dq_out[b] = dq_t[b].astype(BF16)
                dq_copy(b).start()

            return 0

        lax.fori_loop(0, NZ, tile_step, 0)
        for j in range(CB):
            row = c * CB + j
            kv_out[row, pl.ds(0, T), :] = (dkv[pl.ds(j * T, T), pl.ds(0, D)] * SCALE).astype(BF16)
            kv_out[row, pl.ds(T, T), :] = dkv[pl.ds(j * T, T), pl.ds(D, D)].astype(BF16)

            @pl.when(row != s)
            def _():
                dkv_copy(row).start()

        return 0

    lax.fori_loop(0, NCH, chunk_step, 0)

    def wait_o(b):
        pltpu.make_async_remote_copy(
            src_ref=o_out.at[b],
            dst_ref=o_in.at[b],
            send_sem=o_send.at[z],
            recv_sem=o_recv.at[b],
            device_id=device(group_row(s, z, b), b),
            device_id_type=MESH,
        ).wait_recv()

    def wait_dq(b):
        pltpu.make_async_remote_copy(
            src_ref=dq_out.at[b],
            dst_ref=dq_in.at[b],
            send_sem=dq_send.at[z],
            recv_sem=dq_recv.at[b],
            device_id=device(group_row(s, z, b), b),
            device_id_type=MESH,
        ).wait_recv()

    highs = [stats[z, j, pl.ds(0, 1), :] for j in range(NZ)]
    high = functools.reduce(jnp.maximum, highs)
    total = sum(stats[z, j, pl.ds(1, 1), :] * jnp.exp2(highs[j] - high) for j in range(NZ))
    out_t[z] = out_t[z] * coef[z]

    def add_o(i, _):
        b = (z + i) % NZ
        wait_o(b)
        fac = jnp.exp2(stats[z, b, pl.ds(0, 1), :] - high) / total
        out_t[z] += o_in[b].astype(F32) * fac
        return 0

    lax.fori_loop(1, NZ, add_o, 0)
    for h in range(HEADS):
        att_ref[:, pl.ds(h * D, D)] = out_t[z, :, pl.ds(h * T, T)].T.astype(BF16)

    def add_dq(i, _):
        b = (z + i) % NZ
        wait_dq(b)
        dq_t[z] += dq_in[b].astype(F32)
        return 0

    lax.fori_loop(1, NZ, add_dq, 0)
    for h in range(HEADS):
        gq_ref[:, pl.ds(h * D, D)] = (dq_t[z, :, pl.ds(h * T, T)] * SCALE).T.astype(BF16)

    dkv[:, pl.ds(0, D)] = kv_out[s].astype(F32)

    def add_kv(i, _):
        row = (s + i) % NS
        pltpu.make_async_remote_copy(
            src_ref=kv_out.at[row],
            dst_ref=kv_in.at[row],
            send_sem=dkv_send.at[s],
            recv_sem=dkv_recv.at[row],
            device_id=device(row, z),
            device_id_type=MESH,
        ).wait_recv()
        dkv[:, pl.ds(0, D)] += kv_in[row].astype(F32)
        return 0

    lax.fori_loop(1, NS, add_kv, 0)
    gk_ref[...] = dkv[pl.ds(0, T), pl.ds(0, D)].astype(BF16)
    gv_ref[...] = dkv[pl.ds(T, T), pl.ds(0, D)].astype(BF16)

    lax.fori_loop(1, NS // 2, lambda i, _: (kv_copy(i).wait_send(), 0)[1], 0)
    lax.fori_loop(0, NS // 2, lambda i, _: (pass_copy(i).wait_send(), 0)[1], 0)
    lax.fori_loop(1, NZ, lambda i, _: (q_copy(i).wait_send(), 0)[1], 0)

    def drain_group(i, _):
        b = (z + i) % NZ
        o_copy(b).wait_send()
        dq_copy(b).wait_send()
        return 0

    lax.fori_loop(1, NZ, drain_group, 0)

    def drain_stats(b, _):
        lax.fori_loop(1, NZ, lambda j, _: (st_copy(b, j).wait_send(), 0)[1], 0)
        return 0

    lax.fori_loop(0, NZ, drain_stats, 0)
    lax.fori_loop(1, NS, lambda i, _: (dkv_copy((s + i) % NS).wait_send(), 0)[1], 0)


def shards(queries, keys, values, grad_out):
    vmem = pl.BlockSpec(memory_space=pltpu.VMEM)
    dma = pltpu.SemaphoreType.DMA
    return pl.pallas_call(
        kernel,
        out_shape=(
            jax.ShapeDtypeStruct((T, QC), BF16),
            jax.ShapeDtypeStruct((T, QC), BF16),
            jax.ShapeDtypeStruct((T, D), BF16),
            jax.ShapeDtypeStruct((T, D), BF16),
        ),
        in_specs=[vmem] * 4,
        out_specs=(vmem,) * 4,
        scratch_shapes=[
            pltpu.VMEM((NS, 2 * T, D), BF16),
            pltpu.VMEM((NCH, 2 * D, CK), BF16),
            pltpu.VMEM((NZ, 2 * QC, D), BF16),
            pltpu.VMEM((NZ, 2 * D, QC), BF16),
            pltpu.VMEM((NCH, CK, QC), F32),
            pltpu.VMEM((MAXP, CK, QC), BF16),
            pltpu.VMEM((NZ, D, QC), F32),
            pltpu.VMEM((NZ, D, QC), F32),
            pltpu.VMEM((NZ, NZ, 8, QC), F32),
            pltpu.VMEM((NZ, 1, QC), F32),
            pltpu.VMEM((NZ, 1, QC), F32),
            pltpu.VMEM((CK, 2 * D), F32),
            pltpu.VMEM((NS, 2 * T, D), BF16),
            pltpu.VMEM((NS, 2 * T, D), BF16),
            pltpu.VMEM((NZ, D, QC), BF16),
            pltpu.VMEM((NZ, D, QC), BF16),
            pltpu.VMEM((NZ, D, QC), BF16),
            pltpu.VMEM((NZ, D, QC), BF16),
            dma((NS // 2,)),
            dma((NS,)),
            dma((NS // 2,)),
            dma((NZ,)),
            dma((NZ,)),
            dma((NZ, NZ)),
            dma((NZ, NZ)),
            dma((NZ,)),
            dma((NZ,)),
            dma((NZ,)),
            dma((NZ,)),
            dma((NS,)),
            dma((NS,)),
        ],
        compiler_params=pltpu.CompilerParams(
            collective_id=0, has_side_effects=True, vmem_limit_bytes=60 * 1024 * 1024
        ),
        cost_estimate=pl.CostEstimate(
            flops=10_000_000_000, bytes_accessed=10_000_000, transcendentals=6_500_000
        ),
    )(queries, keys, values, grad_out)


def solution(mesh):
    spec = P(("ctxa", "ctxb"), None)
    return jax.shard_map(
        shards,
        mesh=mesh,
        in_specs=(spec,) * 4,
        out_specs=(spec,) * 4,
        check_vma=False,
    )
```

```python
import functools
import math

import jax
import jax.numpy as jnp
from jax import lax
from jax.experimental import pallas as pl
from jax.experimental.pallas import tpu as pltpu
from jax.sharding import PartitionSpec as P

MESH = pl.DeviceIdType.MESH
BF16 = jnp.bfloat16
F32 = jnp.float32

HEADS = 6
D = 128
T = 128
QC = HEADS * T
NS = 32
NZ = 4
CB = 2
CK = CB * T
NCH = NS // CB
MAXP = 36
SCALE = D ** -0.5
C2 = SCALE * math.log2(math.e)
LOW = -1e30


def group_row(s, z, b):
    flip = (b + z) % 2
    return s + flip * (NS - 1 - 2 * s)


def chunks_of(s, z, b):
    seen = group_row(s, z, b) + (b >= z).astype(jnp.int32)
    return (seen + CB - 1) // CB


def base_of(s, z, b):
    total = jnp.int32(0)
    for other in range(NZ):
        total = total + jnp.where(other < b, chunks_of(s, z, jnp.int32(other)), 0)
    return total


def transpose_heads(src, dst, b):
    for h in range(HEADS):
        dst[b, :, pl.ds(h * T, T)] = src[b, pl.ds(h * T, T), :].T


def transpose_rows(src, dst, row):
    for lane in range(CB):

        @pl.when(row % CB == lane)
        def _():
            dst[row // CB, :, pl.ds(lane * T, T)] = src[row].T


def chunk_rows(src, c):
    return src[pl.ds(c * CB, CB)].reshape(CK, D)


def score_block(s, z, b, kb, qt, scores):
    count = chunks_of(s, z, b)
    q_block = group_row(s, z, b) * NZ + b

    def score(c):
        return jnp.dot(chunk_rows(kb, c), qt[b], preferred_element_type=F32)

    def top(x):
        return jnp.max(x.reshape(CK // 8, 8, QC), axis=0)

    def score_step(c, high):
        x = score(c)
        scores[c] = x
        return jnp.maximum(high, top(x))

    def last_step(c, high):
        x = score(c)
        row = lax.broadcasted_iota(jnp.int32, (CK, QC), 0)
        col = lax.broadcasted_iota(jnp.int32, (CK, QC), 1)
        key_pos = ((c * CB + row // T) * NZ + z) * T + row % T
        q_pos = q_block * T + col % T
        x = jnp.where(key_pos <= q_pos, x, LOW)
        scores[c] = x
        return jnp.maximum(high, top(x))

    high = jnp.full((8, QC), LOW, F32)
    high = lax.fori_loop(0, count - 1, score_step, high)
    high = lax.fori_loop(jnp.maximum(count - 1, 0), count, last_step, high)
    return jnp.max(high, axis=0, keepdims=True) * C2


def prob_block(s, z, b, row_max, vt, scores, probs, out_t):
    count = chunks_of(s, z, b)
    base = base_of(s, z, b)
    out_t[b] = jnp.zeros((D, QC), F32)

    def prob_step(c, total):
        p = jnp.exp2(scores[c] * C2 - row_max)
        total = total + jnp.sum(p.reshape(CK // 8, 8, QC), axis=0)
        pb = p.astype(BF16)
        probs[base + c] = pb
        out_t[b] += jnp.dot(vt[c], pb, preferred_element_type=F32)
        return total

    total = lax.fori_loop(0, count, prob_step, jnp.zeros((8, QC), F32))
    return jnp.sum(total, axis=0, keepdims=True)


def stat_block(z, b, row_max, row_sum, gt, out_t, stats):
    part_delta = jnp.sum(gt[b].astype(F32) * out_t[b], axis=0, keepdims=True)
    stats[b, z] = jnp.concatenate(
        [row_max, row_sum, part_delta, jnp.zeros((5, QC), F32)], axis=0
    )


def merge_stats(z, b, stats, coef, delta):
    highs = [stats[b, j, pl.ds(0, 1), :] for j in range(NZ)]
    high = functools.reduce(jnp.maximum, highs)
    facs = [jnp.exp2(x - high) for x in highs]
    total = sum(stats[b, j, pl.ds(1, 1), :] * facs[j] for j in range(NZ))
    inv = 1.0 / total
    coef[b] = jnp.exp2(stats[b, z, pl.ds(0, 1), :] - high) * inv
    delta[b] = sum(stats[b, j, pl.ds(2, 1), :] * facs[j] for j in range(NZ)) * inv


def backward_tile(s, z, b, c, vb, kt, qh, gh, gt, probs, coef, delta, dq_t, dkv):
    base = base_of(s, z, b)
    dw = jnp.dot(chunk_rows(vb, c), gt[b], preferred_element_type=F32)
    w = probs[base + c].astype(F32) * coef[b]
    ds = (w * (dw - delta[b])).astype(BF16)
    wb = w.astype(BF16)
    dkv[c, :, pl.ds(0, D)] += jnp.dot(ds, qh[b], preferred_element_type=F32)
    dkv[c, :, pl.ds(D, D)] += jnp.dot(wb, gh[b], preferred_element_type=F32)
    dq_t[b] += jnp.dot(kt[c], ds, preferred_element_type=F32)


def kernel(
    q_ref, k_ref, v_ref, g_ref,
    att_ref, gq_ref, gk_ref, gv_ref,
    kb, vb, kt, vt, qh, gh, qt, gt, scores, probs, out_t, dq_t, stats, coef, delta, dkv,
    sib_in, kv_out, kv_in, o_out, o_in, dq_out, dq_in,
    k_send, k_recv, kf_send, v_send, v_recv, vf_send, q_send, q_recv, g_send, g_recv,
    st_send, st_recv, o_send, o_recv, dq_send, dq_recv, sib_send, sib_recv, dkv_send, dkv_recv,
):
    ia = lax.axis_index("ctxa")
    ib = lax.axis_index("ctxb")
    z = ib % NZ
    s = ia * 2 + ib // NZ
    core = ia % 2
    x = (ia // 2) % 4
    y = (ia // 8) * 2 + ib // NZ
    sibling = s + 2 - 4 * core
    chip = (s // 4) * 2 + s % 2

    def device(row, plane):
        return (row // 2, (row % 2) * NZ + plane)

    def remote(src, dst, send, recv, row, plane):
        return pltpu.make_async_remote_copy(
            src_ref=src, dst_ref=dst, send_sem=send, recv_sem=recv,
            device_id=device(row, plane), device_id_type=MESH,
        )

    def each(low, high, step):
        lax.fori_loop(low, high, lambda i, _: (step(i), 0)[1], 0)

    def moved(i, sign):
        nx = (x + sign * (i % 4) + 4) % 4
        ny = (y + sign * (i // 4) + 4) % 4
        return (ny // 2) * 16 + nx * 4 + core * 2 + ny % 2

    def member(i):
        b = (z + i) % NZ
        return b, group_row(s, z, b)

    barrier = pltpu.get_barrier_semaphore()

    def signal(row, plane):
        pl.semaphore_signal(
            barrier, inc=1, device_id=device(row, plane), device_id_type=MESH
        )

    each(1, NS, lambda i: signal((s + i) % NS, z))
    for i in range(1, NZ):
        b, row = member(i)
        signal(row, b)

    kb[s] = k_ref[...]
    vb[s] = v_ref[...]
    for h in range(HEADS):
        qh[z, pl.ds(h * T, T), :] = q_ref[:, pl.ds(h * D, D)]
        gh[z, pl.ds(h * T, T), :] = g_ref[:, pl.ds(h * D, D)]

    pl.semaphore_wait(barrier, NS - 1 + NZ - 1)

    def k_copy(i):
        return remote(kb.at[s], kb.at[s], k_send.at[i], k_recv.at[s], moved(i, 1), z)

    def v_copy(i):
        return remote(vb.at[s], vb.at[s], v_send.at[i], v_recv.at[s], moved(i, 1), z)

    def q_copy(i):
        b, row = member(i)
        return remote(qh.at[z], qh.at[z], q_send.at[i], q_recv.at[z], row, b)

    def g_copy(i):
        b, row = member(i)
        return remote(gh.at[z], gh.at[z], g_send.at[i], g_recv.at[z], row, b)

    def k_pass(i):
        row = moved(i, -1)
        return remote(kb.at[row], kb.at[row], kf_send.at[i], k_recv.at[row], sibling, z)

    def v_pass(i):
        row = moved(i, -1)
        return remote(vb.at[row], vb.at[row], vf_send.at[i], v_recv.at[row], sibling, z)

    q_copy(2).start()
    each(1, NS // 2, lambda i: k_copy(i).start())
    q_copy(1).start()
    q_copy(3).start()
    each(1, NS // 2, lambda i: v_copy(i).start())
    each(1, NZ, lambda i: g_copy(i).start())

    transpose_heads(qh, qt, z)
    transpose_heads(gh, gt, z)
    dkv[...] = jnp.zeros((NCH, CK, 2 * D), F32)
    dq_t[...] = jnp.zeros((NZ, D, QC), F32)

    def gather(buf, flipped, copy, send, recv):
        def wait(row):
            remote(buf.at[row], buf.at[row], send.at[0], recv.at[row], sibling, z).wait_recv()

        def near(i):
            row = moved(i, -1)

            @pl.when(i > 0)
            def _():
                wait(row)

            copy(i).start()
            transpose_rows(buf, flipped, row)

        def far(i):
            row = moved(i, -1) + 2 - 4 * core
            wait(row)
            transpose_rows(buf, flipped, row)

        each(0, NS // 2, near)
        each(0, NS // 2, far)

    gather(kb, kt, k_pass, k_send, k_recv)

    def st_copy(b, i):
        p, row = member(i)
        return remote(stats.at[b, z], stats.at[b, z], st_send.at[b, i], st_recv.at[b, z], row, p)

    def o_copy(b):
        return remote(
            o_out.at[b], o_in.at[z], o_send.at[b], o_recv.at[z], group_row(s, z, b), b
        )

    def dq_copy(b):
        return remote(
            dq_out.at[b], dq_in.at[z], dq_send.at[b], dq_recv.at[z], group_row(s, z, b), b
        )

    def forward_step(i):
        b = (z + i + (i == 2).astype(jnp.int32) - (i == 3).astype(jnp.int32)) % NZ
        row = group_row(s, z, b)

        @pl.when(i > 0)
        def _():
            remote(qh.at[b], qh.at[b], q_send.at[0], q_recv.at[b], row, b).wait_recv()
            transpose_heads(qh, qt, b)

        row_max = score_block(s, z, b, kb, qt, scores)

        @pl.when(i == 0)
        def _():
            gather(vb, vt, v_pass, v_send, v_recv)

        row_sum = prob_block(s, z, b, row_max, vt, scores, probs, out_t)

        @pl.when(i > 0)
        def _():
            o_out[b] = out_t[b].astype(BF16)
            o_copy(b).start()
            remote(gh.at[b], gh.at[b], g_send.at[0], g_recv.at[b], row, b).wait_recv()
            transpose_heads(gh, gt, b)

        stat_block(z, b, row_max, row_sum, gt, out_t, stats)
        each(1, NZ, lambda j: st_copy(b, j).start())

    each(0, NZ, forward_step)

    def merge(b):
        def wait(j):
            p, row = member(j)
            remote(
                stats.at[b, p], stats.at[b, p], st_send.at[b, 0], st_recv.at[b, p], row, p
            ).wait_recv()

        each(1, NZ, wait)
        merge_stats(z, b, stats, coef, delta)

    def tile(b, c):
        backward_tile(s, z, b, c, vb, kt, qh, gh, gt, probs, coef, delta, dq_t, dkv)

    def send_dq(b):
        dq_out[b] = dq_t[b].astype(BF16)
        dq_copy(b).start()

    def first_group(i):
        b = (z + 1 + 2 * i) % NZ
        merge(b)
        each(0, chunks_of(s, z, b), lambda c: tile(b, c))
        send_dq(b)

    each(0, 2, first_group)
    merge((z + 2) % NZ)
    merge(z)

    def chunk_at(i):
        ny = (y // 2 + i // 8) % 2
        nx = (x + (i // 2) % 4) % 4
        return ny * 8 + nx * 2 + i % 2

    def sib_copy(i):
        c = chunk_at(i)
        return remote(
            dkv.at[c, pl.ds((1 - core) * T, T), :], sib_in.at[i], sib_send.at[i], sib_recv.at[i], sibling, z
        )

    def dkv_copy(i):
        row = chunk_at(i) * CB + core
        return remote(kv_out.at[i], kv_in.at[chip], dkv_send.at[i], dkv_recv.at[chip], row, z)

    def finish(i):
        c = chunk_at(i)
        sib_copy(i).wait_recv()
        terms = dkv[c, pl.ds(core * T, T), :] + sib_in[i]
        kv_out[i, pl.ds(0, T), :] = (terms[:, :D] * SCALE).astype(BF16)
        kv_out[i, pl.ds(T, T), :] = terms[:, D:].astype(BF16)

        @pl.when(c * CB + core != s)
        def _():
            dkv_copy(i).start()

        @pl.when(c * CB + core == s)
        def _():
            kv_in[chip] = kv_out[i]

    def chunk_step(i):
        c = chunk_at(i)

        def one(j):
            b = (z + 2 * j) % NZ

            @pl.when(c < chunks_of(s, z, b))
            def _():
                tile(b, c)

        each(0, 2, one)
        sib_copy(i).start()

        @pl.when(i > 0)
        def _():
            finish(i - 1)

    each(0, NCH, chunk_step)
    send_dq((z + 2) % NZ)
    finish(NCH - 1)

    highs = [stats[z, j, pl.ds(0, 1), :] for j in range(NZ)]
    high = functools.reduce(jnp.maximum, highs)
    total = sum(stats[z, j, pl.ds(1, 1), :] * jnp.exp2(highs[j] - high) for j in range(NZ))
    out_t[z] = out_t[z] * coef[z]

    def add_o(i):
        b, row = member(i)
        remote(o_out.at[b], o_in.at[b], o_send.at[z], o_recv.at[b], row, b).wait_recv()
        fac = jnp.exp2(stats[z, b, pl.ds(0, 1), :] - high) / total
        out_t[z] += o_in[b].astype(F32) * fac

    each(1, NZ, add_o)
    for h in range(HEADS):
        att_ref[:, pl.ds(h * D, D)] = out_t[z, :, pl.ds(h * T, T)].T.astype(BF16)

    def add_dq(i):
        b, row = member(i)
        remote(dq_out.at[b], dq_in.at[b], dq_send.at[z], dq_recv.at[b], row, b).wait_recv()
        dq_t[z] += dq_in[b].astype(F32)

    each(1, NZ, add_dq)
    for h in range(HEADS):
        gq_ref[:, pl.ds(h * D, D)] = (dq_t[z, :, pl.ds(h * T, T)] * SCALE).T.astype(BF16)

    def add_kv(i, total):
        other = (i // 2) * 4 + (s % 2) * 2 + i % 2

        @pl.when(other != s)
        def _():
            remote(
                kv_out.at[0], kv_in.at[i], dkv_send.at[0], dkv_recv.at[i], other, z
            ).wait_recv()

        return total + kv_in[i].astype(F32)

    total = lax.fori_loop(0, NS // 2, add_kv, jnp.zeros((2 * T, D), F32))
    gk_ref[...] = total[:T].astype(BF16)
    gv_ref[...] = total[T:].astype(BF16)

    each(1, NS // 2, lambda i: k_copy(i).wait_send())
    each(1, NS // 2, lambda i: v_copy(i).wait_send())
    each(0, NS // 2, lambda i: k_pass(i).wait_send())
    each(0, NS // 2, lambda i: v_pass(i).wait_send())

    def drain_group(i):
        b, _ = member(i)
        q_copy(i).wait_send()
        g_copy(i).wait_send()
        o_copy(b).wait_send()
        dq_copy(b).wait_send()

    each(1, NZ, drain_group)
    each(0, NZ, lambda b: each(1, NZ, lambda j: st_copy(b, j).wait_send()))

    def drain_kv(i):
        sib_copy(i).wait_send()

        @pl.when(chunk_at(i) * CB + core != s)
        def _():
            dkv_copy(i).wait_send()

    each(0, NCH, drain_kv)


def shards(queries, keys, values, grad_out):
    vmem = pl.BlockSpec(memory_space=pltpu.VMEM)
    dma = pltpu.SemaphoreType.DMA
    return pl.pallas_call(
        kernel,
        out_shape=(
            jax.ShapeDtypeStruct((T, QC), BF16),
            jax.ShapeDtypeStruct((T, QC), BF16),
            jax.ShapeDtypeStruct((T, D), BF16),
            jax.ShapeDtypeStruct((T, D), BF16),
        ),
        in_specs=[vmem] * 4,
        out_specs=(vmem,) * 4,
        scratch_shapes=[
            pltpu.VMEM((NS, T, D), BF16),
            pltpu.VMEM((NS, T, D), BF16),
            pltpu.VMEM((NCH, D, CK), BF16),
            pltpu.VMEM((NCH, D, CK), BF16),
            pltpu.VMEM((NZ, QC, D), BF16),
            pltpu.VMEM((NZ, QC, D), BF16),
            pltpu.VMEM((NZ, D, QC), BF16),
            pltpu.VMEM((NZ, D, QC), BF16),
            pltpu.VMEM((NCH, CK, QC), F32),
            pltpu.VMEM((MAXP, CK, QC), BF16),
            pltpu.VMEM((NZ, D, QC), F32),
            pltpu.VMEM((NZ, D, QC), F32),
            pltpu.VMEM((NZ, NZ, 8, QC), F32),
            pltpu.VMEM((NZ, 1, QC), F32),
            pltpu.VMEM((NZ, 1, QC), F32),
            pltpu.VMEM((NCH, CK, 2 * D), F32),
            pltpu.VMEM((NCH, T, 2 * D), F32),
            pltpu.VMEM((NCH, 2 * T, D), BF16),
            pltpu.VMEM((NS // 2, 2 * T, D), BF16),
            pltpu.VMEM((NZ, D, QC), BF16),
            pltpu.VMEM((NZ, D, QC), BF16),
            pltpu.VMEM((NZ, D, QC), BF16),
            pltpu.VMEM((NZ, D, QC), BF16),
            dma((NS // 2,)),
            dma((NS,)),
            dma((NS // 2,)),
            dma((NS // 2,)),
            dma((NS,)),
            dma((NS // 2,)),
            dma((NZ,)),
            dma((NZ,)),
            dma((NZ,)),
            dma((NZ,)),
            dma((NZ, NZ)),
            dma((NZ, NZ)),
            dma((NZ,)),
            dma((NZ,)),
            dma((NZ,)),
            dma((NZ,)),
            dma((NCH,)),
            dma((NCH,)),
            dma((NCH,)),
            dma((NS // 2,)),
        ],
        compiler_params=pltpu.CompilerParams(
            collective_id=0, has_side_effects=True, vmem_limit_bytes=60 * 1024 * 1024
        ),
        cost_estimate=pl.CostEstimate(
            flops=10_000_000_000, bytes_accessed=10_000_000, transcendentals=6_500_000
        ),
    )(queries, keys, values, grad_out)


def solution(mesh):
    spec = P(("ctxa", "ctxb"), None)
    return jax.shard_map(
        shards,
        mesh=mesh,
        in_specs=(spec,) * 4,
        out_specs=(spec,) * 4,
        check_vma=False,
    )
```

```python
import functools
import math

import jax
import jax.numpy as jnp
from jax import lax
from jax.experimental import pallas as pl
from jax.experimental.pallas import tpu as pltpu
from jax.sharding import PartitionSpec as P

MESH = pl.DeviceIdType.MESH
BF16 = jnp.bfloat16
F32 = jnp.float32

HEADS = 6
D = 128
T = 128
QC = HEADS * T
NS = 32
NZ = 4
CB = 2
CK = CB * T
NCH = NS // CB
ROUNDS = NS // 4
MAXP = 36
SCALE = D ** -0.5
C2 = SCALE * math.log2(math.e)
LOW = -1e30


def group_row(s, z, b):
    flip = (b + z) % 2
    return s + flip * (NS - 1 - 2 * s)


def chunks_of(s, z, b):
    seen = group_row(s, z, b) + (b >= z).astype(jnp.int32)
    return (seen + CB - 1) // CB


def base_of(s, z, b):
    total = jnp.int32(0)
    for other in range(NZ):
        total = total + jnp.where(other < b, chunks_of(s, z, jnp.int32(other)), 0)
    return total


def transpose_heads(src, dst, b):
    for h in range(HEADS):
        dst[b, :, pl.ds(h * T, T)] = src[b, pl.ds(h * T, T), :].T


def transpose_rows(src, dst, row):
    dst[:, pl.ds(pl.multiple_of(row * T, T), T)] = src[row].T


def rows_of(src, c, size):
    return src[pl.ds(c * CB, size * CB)].reshape(size * CK, D)


def lanes_of(src, c, size):
    return src[:, pl.ds(pl.multiple_of(c * CK, CK), size * CK)]


def tiles(count, step, carry):
    big = count // 4
    carry = lax.fori_loop(0, big, lambda i, now: step(4 * i, 4, now), carry)
    carry = lax.fori_loop(0, (count % 4) // 2, lambda i, now: step(4 * big, 2, now), carry)
    return lax.fori_loop(0, count % 2, lambda i, now: step(count - 1, 1, now), carry)


def score_block(s, z, b, kb, qt, scores):
    count = chunks_of(s, z, b)
    q_block = group_row(s, z, b) * NZ + b

    def keep(c, size, high, x):
        scores[pl.ds(c, size)] = x.reshape(size, CK, QC)
        return jnp.maximum(high, jnp.max(x.reshape(size * CK // 8, 8, QC), axis=0))

    def score(c, size):
        return jnp.dot(rows_of(kb, c, size), qt[b], preferred_element_type=F32)

    def plain(c, size, high):
        return keep(c, size, high, score(c, size))

    def masked(c, size, high):
        row = lax.broadcasted_iota(jnp.int32, (size * CK, QC), 0)
        col = lax.broadcasted_iota(jnp.int32, (size * CK, QC), 1)
        key_pos = ((c * CB + row // T) * NZ + z) * T + row % T
        q_pos = q_block * T + col % T
        return keep(c, size, high, jnp.where(key_pos <= q_pos, score(c, size), LOW))

    odd = count % 2
    even = ((count > 0) & (odd == 0)).astype(jnp.int32)
    high = jnp.full((8, QC), LOW, F32)
    high = tiles(count - odd - 2 * even, plain, high)
    high = lax.fori_loop(0, even, lambda i, now: masked(count - 2, 2, now), high)
    high = lax.fori_loop(0, odd, lambda i, now: masked(count - 1, 1, now), high)
    return jnp.max(high, axis=0, keepdims=True) * C2


def prob_block(s, z, b, row_max, vt, scores, probs, out_t):
    base = base_of(s, z, b)
    out_t[b] = jnp.zeros((D, QC), F32)

    def step(c, size, total):
        p = jnp.exp2(scores[pl.ds(c, size)].reshape(size * CK, QC) * C2 - row_max)
        total = total + jnp.sum(p.reshape(size * CK // 8, 8, QC), axis=0)
        pb = p.astype(BF16)
        probs[pl.ds(base + c, size)] = pb.reshape(size, CK, QC)
        out_t[b] += jnp.dot(lanes_of(vt, c, size), pb, preferred_element_type=F32)
        return total

    total = tiles(chunks_of(s, z, b), step, jnp.zeros((8, QC), F32))
    return jnp.sum(total, axis=0, keepdims=True)


def by_head(row):
    parts = [row[:, h * T : (h + 1) * T] for h in range(HEADS)]
    return jnp.concatenate(parts + [jnp.zeros((8 - HEADS, T), F32)], axis=0)


def in_line(rows):
    return jnp.concatenate([rows[h : h + 1] for h in range(HEADS)], axis=1)


def stat_block(z, b, row_max, row_sum, gt, out_t, stats, top):
    part_delta = jnp.sum(gt[b].astype(F32) * out_t[b], axis=0, keepdims=True)
    row_sum = jnp.maximum(row_sum, 1e-37)
    top[b] = row_max
    stats[b, z, pl.ds(0, 8), :] = by_head(row_max + jnp.log2(row_sum))
    stats[b, z, pl.ds(8, 8), :] = by_head(part_delta / row_sum)
    stats[b, z, pl.ds(16, 8), :] = by_head(row_max)


def merge_stats(b, stats, top, coef, delta, parts):
    logs = [stats[b, j, pl.ds(0, 8), :] for j in range(NZ)]
    high = functools.reduce(jnp.maximum, logs)
    log_total = high + jnp.log2(sum(jnp.exp2(x - high) for x in logs))
    shares = [jnp.exp2(x - log_total) for x in logs]
    coef[b] = jnp.exp2(top[b] - in_line(log_total))
    if parts is not None:
        for j in range(NZ):
            parts[j] = in_line(jnp.exp2(stats[b, j, pl.ds(16, 8), :] - log_total))
    delta[b] = in_line(sum(stats[b, j, pl.ds(8, 8), :] * shares[j] for j in range(NZ)))


def backward_tile(s, z, b, c, size, vb, kt, qh, gh, gt, probs, coef, delta, dq_t, dkv):
    base = base_of(s, z, b)
    dw = jnp.dot(rows_of(vb, c, size), gt[b], preferred_element_type=F32)
    w = probs[pl.ds(base + c, size)].reshape(size * CK, QC).astype(F32) * coef[b]
    ds = (w * (dw - delta[b])).astype(BF16)
    wb = w.astype(BF16)
    rows = pl.ds(pl.multiple_of(c * CK, CK), size * CK)
    dkv[rows, pl.ds(0, D)] += jnp.dot(ds, qh[b], preferred_element_type=F32)
    dkv[rows, pl.ds(D, D)] += jnp.dot(wb, gh[b], preferred_element_type=F32)
    dq_t[b] += jnp.dot(lanes_of(kt, c, size), ds, preferred_element_type=F32)


def kernel(
    q_ref, k_ref, v_ref, g_ref,
    att_ref, gq_ref, gk_ref, gv_ref,
    kb, vb, kt, vt, qh, gh, qt, gt, scores, probs, out_t, dq_t, stats, top, coef, delta, dkv,
    sib_in, kv_out, kv_in, q_mid, g_mid, o_out, o_in, part_coef, dq_out, dq_in,
    k_send, k_recv, kf_send, v_send, v_recv, vf_send, q_send, q_recv, qm_recv, qp_send, g_send, g_recv, gm_recv, gp_send,
    st_send, st_recv, o_send, o_recv, dq_send, dq_recv, sib_send, sib_recv, dkv_send, dkv_recv,
):
    ia = lax.axis_index("ctxa")
    ib = lax.axis_index("ctxb")
    z = ib % NZ
    s = ia * 2 + ib // NZ
    core = ia % 2
    x = (ia // 2) % 4
    y = (ia // 8) * 2 + ib // NZ
    sibling = s + 2 - 4 * core
    mirror = NS - 1 - s
    chip = (s // 4) * 2 + s % 2

    def device(row, plane):
        return (row // 2, (row % 2) * NZ + plane)

    def remote(src, dst, send, recv, row, plane):
        return pltpu.make_async_remote_copy(
            src_ref=src, dst_ref=dst, send_sem=send, recv_sem=recv,
            device_id=device(row, plane), device_id_type=MESH,
        )

    def each(low, high, step):
        lax.fori_loop(low, high, lambda i, _: (step(i), 0)[1], 0)

    def moved(i, sign):
        nx = (x + sign * (i % 4) + 4) % 4
        ny = (y + sign * (i // 4) + 4) % 4
        return (ny // 2) * 16 + nx * 4 + core * 2 + ny % 2

    def member(i):
        b = (z + i) % NZ
        return b, group_row(s, z, b)

    barrier = pltpu.get_barrier_semaphore()

    def signal(row, plane):
        pl.semaphore_signal(
            barrier, inc=1, device_id=device(row, plane), device_id_type=MESH
        )

    each(1, NS // 2, lambda i: signal(moved(i, 1), z))
    signal(sibling, z)
    for i in range(1, NZ):
        b, row = member(i)
        signal(row, b)
    signal(mirror, z)
    signal(s, (z + 1) % NZ)
    signal(s, (z + 3) % NZ)

    kb[s] = k_ref[...]
    vb[s] = v_ref[...]
    for h in range(HEADS):
        qh[z, pl.ds(h * T, T), :] = q_ref[:, pl.ds(h * D, D)]
        gh[z, pl.ds(h * T, T), :] = g_ref[:, pl.ds(h * D, D)]

    pl.semaphore_wait(barrier, NS // 2 - 1 + 1 + NZ - 1 + 3)

    def k_copy(i):
        return remote(kb.at[s], kb.at[s], k_send.at[i], k_recv.at[s], moved(i, 1), z)

    def v_copy(i):
        return remote(vb.at[s], vb.at[s], v_send.at[i], v_recv.at[s], moved(i, 1), z)

    def q_copy(i):
        if i == 0:
            return remote(qh.at[z], q_mid, q_send.at[0], qm_recv, mirror, z)
        return remote(qh.at[z], qh.at[z], q_send.at[1], q_recv.at[z], s, (z + 2) % NZ)

    def g_copy(i):
        if i == 0:
            return remote(gh.at[z], g_mid, g_send.at[0], gm_recv, mirror, z)
        return remote(gh.at[z], gh.at[z], g_send.at[1], g_recv.at[z], s, (z + 2) % NZ)

    def q_pass(i):
        return remote(q_mid, qh.at[z], qp_send.at[i], q_recv.at[z], s, (z + 1 + 2 * i) % NZ)

    def g_pass(i):
        return remote(g_mid, gh.at[z], gp_send.at[i], g_recv.at[z], s, (z + 1 + 2 * i) % NZ)

    def k_pass(i):
        row = moved(i, -1)
        return remote(kb.at[row], kb.at[row], kf_send.at[i], k_recv.at[row], sibling, z)

    def v_pass(i):
        row = moved(i, -1)
        return remote(vb.at[row], vb.at[row], vf_send.at[i], v_recv.at[row], sibling, z)

    q_copy(0).start()
    q_copy(1).start()
    each(1, NS // 2, lambda i: k_copy(i).start())
    each(1, NS // 2, lambda i: v_copy(i).start())
    g_copy(0).start()
    g_copy(1).start()

    transpose_heads(qh, qt, z)
    transpose_heads(gh, gt, z)
    dkv[...] = jnp.zeros((NS * T, 2 * D), F32)
    dq_t[...] = jnp.zeros((NZ, D, QC), F32)

    def gather(buf, flipped, copy, send, recv, between):
        def wait(row):
            remote(buf.at[row], buf.at[row], send.at[0], recv.at[row], sibling, z).wait_recv()

        def near(i):
            row = moved(i, -1)

            @pl.when(i > 0)
            def _():
                wait(row)

            copy(i).start()
            transpose_rows(buf, flipped, row)

        def far(i):
            row = moved(i, -1) + 2 - 4 * core
            wait(row)
            transpose_rows(buf, flipped, row)

        each(0, NS // 2, near)
        between()
        each(0, NS // 2, far)

    def pass_q():
        q_copy(0).wait_recv()
        q_pass(0).start()
        q_pass(1).start()

    def pass_g():
        g_copy(0).wait_recv()
        g_pass(0).start()
        g_pass(1).start()

    gather(kb, kt, k_pass, k_send, k_recv, pass_q)

    def st_copy(b, i):
        p, row = member(i)
        return remote(stats.at[b, z], stats.at[b, z], st_send.at[b, i], st_recv.at[b, z], row, p)

    def o_copy(i):
        b, row = member(i)
        return remote(o_out.at[b], o_in.at[i - 1], o_send.at[i], o_recv.at[i - 1], row, b)

    def dq_copy(i):
        b, row = member(i)
        return remote(dq_out.at[b], dq_in.at[i - 1], dq_send.at[i], dq_recv.at[i - 1], row, b)

    def forward_step(i):
        b = (z + i + (i == 2).astype(jnp.int32) - (i == 3).astype(jnp.int32)) % NZ
        row = group_row(s, z, b)

        @pl.when(i > 0)
        def _():
            remote(qh.at[b], qh.at[b], q_send.at[0], q_recv.at[b], row, b).wait_recv()
            transpose_heads(qh, qt, b)

        row_max = score_block(s, z, b, kb, qt, scores)

        @pl.when(i == 0)
        def _():
            gather(vb, vt, v_pass, v_send, v_recv, pass_g)

        row_sum = prob_block(s, z, b, row_max, vt, scores, probs, out_t)

        @pl.when(i > 0)
        def _():
            o_out[b] = out_t[b].astype(BF16)
            remote(
                o_out.at[b], o_in.at[(b - z + NZ) % NZ - 1], o_send.at[(b - z + NZ) % NZ],
                o_recv.at[(b - z + NZ) % NZ - 1], row, b,
            ).start()
            remote(gh.at[b], gh.at[b], g_send.at[0], g_recv.at[b], row, b).wait_recv()
            transpose_heads(gh, gt, b)

        stat_block(z, b, row_max, row_sum, gt, out_t, stats, top)
        each(1, NZ, lambda j: st_copy(b, j).start())

    each(0, NZ, forward_step)

    def merge(b, parts=None):
        def wait(j):
            p, row = member(j)
            remote(
                stats.at[b, p], stats.at[b, p], st_send.at[b, 0], st_recv.at[b, p], row, p
            ).wait_recv()

        each(1, NZ, wait)
        merge_stats(b, stats, top, coef, delta, parts)

    def tile(b, c, size):
        backward_tile(s, z, b, c, size, vb, kt, qh, gh, gt, probs, coef, delta, dq_t, dkv)

    def send_dq(i):
        b = (z + i) % NZ
        dq_out[b] = dq_t[b].astype(BF16)
        dq_copy(i).start()

    for i in (1, 3):
        b = (z + i) % NZ
        merge(b)
        tiles(chunks_of(s, z, b), lambda c, size, now: (tile(b, c, size), now)[1], 0)
        send_dq(i)

    merge((z + 2) % NZ)
    merge(z, part_coef)

    def round_at(i):
        ny = (y // 2 + i // 4) % 2
        nx = (x + i % 4) % 4
        return ny * 4 + nx

    def core_rows(i, which):
        return pl.ds(pl.multiple_of(round_at(i) * 4 * T + which * 2 * T, 2 * T), 2 * T)

    def sib_copy(i):
        return remote(
            dkv.at[core_rows(i, 1 - core), :], sib_in.at[i], sib_send.at[i], sib_recv.at[i], sibling, z
        )

    def dkv_copy(i, j):
        row = round_at(i) * 4 + core * 2 + j
        return remote(
            kv_out.at[2 * i + j], kv_in.at[chip], dkv_send.at[2 * i + j], dkv_recv.at[chip], row, z
        )

    def finish(i):
        sib_copy(i).wait_recv()
        for j in range(2):
            rows = pl.ds(pl.multiple_of(round_at(i) * 4 * T + core * 2 * T + j * T, T), T)
            terms = dkv[rows, :] + sib_in[i, pl.ds(j * T, T), :]
            kv_out[2 * i + j, pl.ds(0, T), :] = (terms[:, :D] * SCALE).astype(BF16)
            kv_out[2 * i + j, pl.ds(T, T), :] = terms[:, D:].astype(BF16)
            mine = (i == 0) & (y % 2 == j)

            @pl.when(jnp.logical_not(mine))
            def _():
                dkv_copy(i, j).start()

            @pl.when(mine)
            def _():
                kv_in[chip] = kv_out[2 * i + j]

    def round_step(i):
        c = 2 * round_at(i)

        def one(j):
            b = (z + 2 * j) % NZ
            left = chunks_of(s, z, b) - c

            @pl.when(left > 1)
            def _():
                tile(b, c, 2)

            @pl.when(left == 1)
            def _():
                tile(b, c, 1)

        each(0, 2, one)
        sib_copy(i).start()

        @pl.when(i > 0)
        def _():
            finish(i - 1)

    each(0, ROUNDS, round_step)
    send_dq(2)
    finish(ROUNDS - 1)

    for i in range(1, NZ):
        o_copy(i).wait_recv()
    out_t[z] = out_t[z] * coef[z] + sum(
        o_in[i - 1].astype(F32) * part_coef[(z - i + NZ) % NZ] for i in range(1, NZ)
    )
    for h in range(HEADS):
        att_ref[:, pl.ds(h * D, D)] = out_t[z, :, pl.ds(h * T, T)].T.astype(BF16)

    for i in range(1, NZ):
        dq_copy(i).wait_recv()
    dq_t[z] = (dq_t[z] + sum(dq_in[i].astype(F32) for i in range(NZ - 1))) * SCALE
    for h in range(HEADS):
        gq_ref[:, pl.ds(h * D, D)] = dq_t[z, :, pl.ds(h * T, T)].T.astype(BF16)

    def wait_kv(i):
        row = (i // 2) * 4 + core * 2 + i % 2

        @pl.when(i != chip)
        def _():
            remote(kv_out.at[0], kv_in.at[i], dkv_send.at[0], dkv_recv.at[i], row, z).wait_recv()

    each(0, NS // 2, wait_kv)
    for part in range(4):
        rows = pl.ds(part * T // 4, T // 4)
        gk_ref[rows, :] = jnp.sum(kv_in[:, rows, :].astype(F32), axis=0).astype(BF16)
        rows = pl.ds(T + part * T // 4, T // 4)
        gv_ref[pl.ds(part * T // 4, T // 4), :] = jnp.sum(kv_in[:, rows, :].astype(F32), axis=0).astype(BF16)

    each(1, NS // 2, lambda i: k_copy(i).wait_send())
    each(1, NS // 2, lambda i: v_copy(i).wait_send())
    each(0, NS // 2, lambda i: k_pass(i).wait_send())
    each(0, NS // 2, lambda i: v_pass(i).wait_send())

    for i in range(2):
        q_copy(i).wait_send()
        g_copy(i).wait_send()
        q_pass(i).wait_send()
        g_pass(i).wait_send()
    for i in range(1, NZ):
        o_copy(i).wait_send()
        dq_copy(i).wait_send()
    each(0, NZ, lambda b: each(1, NZ, lambda j: st_copy(b, j).wait_send()))

    def drain_kv(i):
        sib_copy(i).wait_send()
        for j in range(2):

            @pl.when((i != 0) | (y % 2 != j))
            def _():
                dkv_copy(i, j).wait_send()

    each(0, ROUNDS, drain_kv)


def shards(queries, keys, values, grad_out):
    vmem = pl.BlockSpec(memory_space=pltpu.VMEM)
    dma = pltpu.SemaphoreType.DMA
    return pl.pallas_call(
        kernel,
        out_shape=(
            jax.ShapeDtypeStruct((T, QC), BF16),
            jax.ShapeDtypeStruct((T, QC), BF16),
            jax.ShapeDtypeStruct((T, D), BF16),
            jax.ShapeDtypeStruct((T, D), BF16),
        ),
        in_specs=[vmem] * 4,
        out_specs=(vmem,) * 4,
        scratch_shapes=[
            pltpu.VMEM((NS, T, D), BF16),
            pltpu.VMEM((NS, T, D), BF16),
            pltpu.VMEM((D, NS * T), BF16),
            pltpu.VMEM((D, NS * T), BF16),
            pltpu.VMEM((NZ, QC, D), BF16),
            pltpu.VMEM((NZ, QC, D), BF16),
            pltpu.VMEM((NZ, D, QC), BF16),
            pltpu.VMEM((NZ, D, QC), BF16),
            pltpu.VMEM((NCH, CK, QC), F32),
            pltpu.VMEM((MAXP, CK, QC), BF16),
            pltpu.VMEM((NZ, D, QC), F32),
            pltpu.VMEM((NZ, D, QC), F32),
            pltpu.VMEM((NZ, NZ, 24, T), F32),
            pltpu.VMEM((NZ, 1, QC), F32),
            pltpu.VMEM((NZ, 1, QC), F32),
            pltpu.VMEM((NZ, 1, QC), F32),
            pltpu.VMEM((NS * T, 2 * D), F32),
            pltpu.VMEM((ROUNDS, 2 * T, 2 * D), F32),
            pltpu.VMEM((NCH, 2 * T, D), BF16),
            pltpu.VMEM((NS // 2, 2 * T, D), BF16),
            pltpu.VMEM((QC, D), BF16),
            pltpu.VMEM((QC, D), BF16),
            pltpu.VMEM((NZ, D, QC), BF16),
            pltpu.VMEM((NZ - 1, D, QC), BF16),
            pltpu.VMEM((NZ, 1, QC), F32),
            pltpu.VMEM((NZ, D, QC), BF16),
            pltpu.VMEM((NZ - 1, D, QC), BF16),
            dma((NS // 2,)),
            dma((NS,)),
            dma((NS // 2,)),
            dma((NS // 2,)),
            dma((NS,)),
            dma((NS // 2,)),
            dma((2,)),
            dma((NZ,)),
            dma(()),
            dma((2,)),
            dma((2,)),
            dma((NZ,)),
            dma(()),
            dma((2,)),
            dma((NZ, NZ)),
            dma((NZ, NZ)),
            dma((NZ,)),
            dma((NZ - 1,)),
            dma((NZ,)),
            dma((NZ - 1,)),
            dma((ROUNDS,)),
            dma((ROUNDS,)),
            dma((NCH,)),
            dma((NS // 2,)),
        ],
        compiler_params=pltpu.CompilerParams(
            collective_id=0, has_side_effects=True, vmem_limit_bytes=60 * 1024 * 1024
        ),
        cost_estimate=pl.CostEstimate(
            flops=10_000_000_000, bytes_accessed=10_000_000, transcendentals=6_500_000
        ),
    )(queries, keys, values, grad_out)


def solution(mesh):
    spec = P(("ctxa", "ctxb"), None)
    return jax.shard_map(
        shards,
        mesh=mesh,
        in_specs=(spec,) * 4,
        out_specs=(spec,) * 4,
        check_vma=False,
    )
```

```python
import functools
import math

import jax
import jax.numpy as jnp
from jax import lax
from jax.experimental import pallas as pl
from jax.experimental.pallas import tpu as pltpu
from jax.sharding import PartitionSpec as P

MESH = pl.DeviceIdType.MESH
BF16 = jnp.bfloat16
F32 = jnp.float32

HEADS = 6
D = 128
T = 128
QC = HEADS * T
NS = 32
NZ = 4
CB = 2
CK = CB * T
NCH = NS // CB
ROUNDS = NS // 4
MAXP = 36
SCALE = D ** -0.5
C2 = SCALE * math.log2(math.e)
LOW = -1e30


def group_row(s, z, b):
    flip = (b + z) % 2
    return s + flip * (NS - 1 - 2 * s)


def chunks_of(s, z, b):
    seen = group_row(s, z, b) + (b >= z).astype(jnp.int32)
    return (seen + CB - 1) // CB


def base_of(s, z, b):
    total = jnp.int32(0)
    for other in range(NZ):
        total = total + jnp.where(other < b, chunks_of(s, z, jnp.int32(other)), 0)
    return total


def transpose_heads(src, dst, b):
    for h in range(HEADS):
        dst[b, :, pl.ds(h * T, T)] = src[b, pl.ds(h * T, T), :].T


def transpose_rows(src, dst, row):
    dst[:, pl.ds(pl.multiple_of(row * T, T), T)] = src[row].T


def rows_of(src, c, size):
    return src[pl.ds(c * CB, size * CB)].reshape(size * CK, D)


def lanes_of(src, c, size):
    return src[:, pl.ds(pl.multiple_of(c * CK, CK), size * CK)]


def tiles(count, step, carry):
    big = count // 4
    carry = lax.fori_loop(0, big, lambda i, now: step(4 * i, 4, now), carry)
    carry = lax.fori_loop(0, (count % 4) // 2, lambda i, now: step(4 * big, 2, now), carry)
    return lax.fori_loop(0, count % 2, lambda i, now: step(count - 1, 1, now), carry)


def score_block(s, z, b, kb, qt, scores):
    count = chunks_of(s, z, b)
    q_block = group_row(s, z, b) * NZ + b

    def keep(c, size, high, x):
        scores[pl.ds(c, size)] = x.reshape(size, CK, QC)
        return jnp.maximum(high, jnp.max(x.reshape(size * CK // 8, 8, QC), axis=0))

    def score(c, size):
        return jnp.dot(rows_of(kb, c, size), qt[b], preferred_element_type=F32)

    def plain(c, size, high):
        return keep(c, size, high, score(c, size))

    def masked(c, size, high):
        row = lax.broadcasted_iota(jnp.int32, (size * CK, QC), 0)
        col = lax.broadcasted_iota(jnp.int32, (size * CK, QC), 1)
        key_pos = ((c * CB + row // T) * NZ + z) * T + row % T
        q_pos = q_block * T + col % T
        return keep(c, size, high, jnp.where(key_pos <= q_pos, score(c, size), LOW))

    odd = count % 2
    even = ((count > 0) & (odd == 0)).astype(jnp.int32)
    high = jnp.full((8, QC), LOW, F32)
    high = tiles(count - odd - 2 * even, plain, high)
    high = lax.fori_loop(0, even, lambda i, now: masked(count - 2, 2, now), high)
    high = lax.fori_loop(0, odd, lambda i, now: masked(count - 1, 1, now), high)
    return jnp.max(high, axis=0, keepdims=True) * C2


def prob_block(s, z, b, row_max, vt, scores, probs, out_t):
    base = base_of(s, z, b)
    out_t[b] = jnp.zeros((D, QC), F32)

    def step(c, size, total):
        p = jnp.exp2(scores[pl.ds(c, size)].reshape(size * CK, QC) * C2 - row_max)
        total = total + jnp.sum(p.reshape(size * CK // 8, 8, QC), axis=0)
        pb = p.astype(BF16)
        probs[pl.ds(base + c, size)] = pb.reshape(size, CK, QC)
        out_t[b] += jnp.dot(lanes_of(vt, c, size), pb, preferred_element_type=F32)
        return total

    total = tiles(chunks_of(s, z, b), step, jnp.zeros((8, QC), F32))
    return jnp.sum(total, axis=0, keepdims=True)


def by_head(row):
    parts = [row[:, h * T : (h + 1) * T] for h in range(HEADS)]
    return jnp.concatenate(parts + [jnp.zeros((8 - HEADS, T), F32)], axis=0)


def in_line(rows):
    return jnp.concatenate([rows[h : h + 1] for h in range(HEADS)], axis=1)


def stat_block(z, b, row_max, row_sum, gt, out_t, stats):
    part_delta = jnp.sum(gt[b].astype(F32) * out_t[b], axis=0, keepdims=True)
    row_sum = jnp.maximum(row_sum, 1e-37)
    stats[b, z, pl.ds(0, 8), :] = by_head(row_max + jnp.log2(row_sum))
    stats[b, z, pl.ds(8, 8), :] = by_head(part_delta / row_sum)
    stats[b, z, pl.ds(16, 8), :] = by_head(row_max)


def merge_stats(b, stats, top, coef, delta, parts):
    logs = [stats[b, j, pl.ds(0, 8), :] for j in range(NZ)]
    high = functools.reduce(jnp.maximum, logs)
    log_total = high + jnp.log2(sum(jnp.exp2(x - high) for x in logs))
    shares = [jnp.exp2(x - log_total) for x in logs]
    coef[b] = jnp.exp2(top[b] - in_line(log_total))
    if parts is not None:
        for j in range(NZ):
            parts[j] = in_line(jnp.exp2(stats[b, j, pl.ds(16, 8), :] - log_total))
    delta[b] = in_line(sum(stats[b, j, pl.ds(8, 8), :] * shares[j] for j in range(NZ)))


def backward_tile(s, z, b, c, size, vb, kt, qh, gh, gt, probs, coef, delta, dq_t, dkv):
    base = base_of(s, z, b)
    dw = jnp.dot(rows_of(vb, c, size), gt[b], preferred_element_type=F32)
    w = probs[pl.ds(base + c, size)].reshape(size * CK, QC).astype(F32) * coef[b]
    ds = (w * (dw - delta[b])).astype(BF16)
    wb = w.astype(BF16)
    rows = pl.ds(pl.multiple_of(c * CK, CK), size * CK)
    dkv[rows, pl.ds(0, D)] += jnp.dot(ds, qh[b], preferred_element_type=F32)
    dkv[rows, pl.ds(D, D)] += jnp.dot(wb, gh[b], preferred_element_type=F32)
    dq_t[b] += jnp.dot(lanes_of(kt, c, size), ds, preferred_element_type=F32)


def kernel(
    q_ref, k_ref, v_ref, g_ref,
    att_ref, gq_ref, gk_ref, gv_ref,
    kb, vb, kt, vt, qh, gh, qt, gt, scores, probs, out_t, dq_t, stats, top, sums, coef, delta, dkv,
    sib_in, kv_out, kv_in, q_mid, g_mid, o_out, o_in, part_coef, dq_out, dq_in,
    k_send, k_recv, kf_send, v_send, v_recv, vf_send, q_send, q_recv, qm_recv, qp_send, g_send, g_recv, gm_recv, gp_send,
    st_send, st_recv, o_send, o_recv, dq_send, dq_recv, sib_send, sib_recv, dkv_send, dkv_recv,
):
    ia = lax.axis_index("ctxa")
    ib = lax.axis_index("ctxb")
    z = ib % NZ
    s = ia * 2 + ib // NZ
    core = ia % 2
    x = (ia // 2) % 4
    y = (ia // 8) * 2 + ib // NZ
    sibling = s + 2 - 4 * core
    mirror = NS - 1 - s
    chip = (s // 4) * 2 + s % 2

    def device(row, plane):
        return (row // 2, (row % 2) * NZ + plane)

    def remote(src, dst, send, recv, row, plane):
        return pltpu.make_async_remote_copy(
            src_ref=src, dst_ref=dst, send_sem=send, recv_sem=recv,
            device_id=device(row, plane), device_id_type=MESH,
        )

    def each(low, high, step):
        lax.fori_loop(low, high, lambda i, _: (step(i), 0)[1], 0)

    def moved(i, sign):
        nx = (x + sign * (i % 4) + 4) % 4
        ny = (y + sign * (i // 4) + 4) % 4
        return (ny // 2) * 16 + nx * 4 + core * 2 + ny % 2

    def member(i):
        b = (z + i) % NZ
        return b, group_row(s, z, b)

    barrier = pltpu.get_barrier_semaphore()

    def signal(row, plane):
        pl.semaphore_signal(
            barrier, inc=1, device_id=device(row, plane), device_id_type=MESH
        )

    each(1, NS // 2, lambda i: signal(moved(i, 1), z))
    signal(sibling, z)
    for i in range(1, NZ):
        b, row = member(i)
        signal(row, b)
    signal(mirror, z)
    signal(s, (z + 1) % NZ)
    signal(s, (z + 3) % NZ)

    kb[s] = k_ref[...]
    vb[s] = v_ref[...]
    for h in range(HEADS):
        qh[z, pl.ds(h * T, T), :] = q_ref[:, pl.ds(h * D, D)]
        gh[z, pl.ds(h * T, T), :] = g_ref[:, pl.ds(h * D, D)]

    pl.semaphore_wait(barrier, NS // 2 - 1 + 1 + NZ - 1 + 3)

    def k_copy(i):
        return remote(kb.at[s], kb.at[s], k_send.at[i], k_recv.at[s], moved(i, 1), z)

    def v_copy(i):
        return remote(vb.at[s], vb.at[s], v_send.at[i], v_recv.at[s], moved(i, 1), z)

    def q_copy(i):
        if i == 0:
            return remote(qh.at[z], q_mid, q_send.at[0], qm_recv, mirror, z)
        return remote(qh.at[z], qh.at[z], q_send.at[1], q_recv.at[z], s, (z + 2) % NZ)

    def g_copy(i):
        if i == 0:
            return remote(gh.at[z], g_mid, g_send.at[0], gm_recv, mirror, z)
        return remote(gh.at[z], gh.at[z], g_send.at[1], g_recv.at[z], s, (z + 2) % NZ)

    def q_pass(i):
        return remote(q_mid, qh.at[z], qp_send.at[i], q_recv.at[z], s, (z + 1 + 2 * i) % NZ)

    def g_pass(i):
        return remote(g_mid, gh.at[z], gp_send.at[i], g_recv.at[z], s, (z + 1 + 2 * i) % NZ)

    def k_pass(i):
        row = moved(i, -1)
        return remote(kb.at[row], kb.at[row], kf_send.at[i], k_recv.at[row], sibling, z)

    def v_pass(i):
        row = moved(i, -1)
        return remote(vb.at[row], vb.at[row], vf_send.at[i], v_recv.at[row], sibling, z)

    q_copy(0).start()
    q_copy(1).start()
    each(1, NS // 2, lambda i: k_copy(i).start())
    each(1, NS // 2, lambda i: v_copy(i).start())
    g_copy(0).start()
    g_copy(1).start()

    transpose_heads(qh, qt, z)
    transpose_heads(gh, gt, z)
    dkv[...] = jnp.zeros((NS * T, 2 * D), F32)
    dq_t[...] = jnp.zeros((NZ, D, QC), F32)

    def gather(buf, flipped, copy, send, recv, between):
        def wait(row):
            remote(buf.at[row], buf.at[row], send.at[0], recv.at[row], sibling, z).wait_recv()

        def near(i):
            row = moved(i, -1)

            @pl.when(i > 0)
            def _():
                wait(row)

            copy(i).start()
            transpose_rows(buf, flipped, row)

        def far(i):
            row = moved(i, -1) + 2 - 4 * core
            wait(row)
            transpose_rows(buf, flipped, row)

        each(0, NS // 2, near)
        between()
        each(0, NS // 2, far)

    def pass_q():
        q_copy(0).wait_recv()
        q_pass(0).start()
        q_pass(1).start()

    def pass_g():
        g_copy(0).wait_recv()
        g_pass(0).start()
        g_pass(1).start()

    gather(kb, kt, k_pass, k_send, k_recv, pass_q)

    def st_copy(b, i):
        p, row = member(i)
        return remote(stats.at[b, z], stats.at[b, z], st_send.at[b, i], st_recv.at[b, z], row, p)

    def o_copy(i):
        b, row = member(i)
        return remote(o_out.at[b], o_in.at[i - 1], o_send.at[i], o_recv.at[i - 1], row, b)

    def dq_copy(i):
        b, row = member(i)
        return remote(dq_out.at[b], dq_in.at[i - 1], dq_send.at[i], dq_recv.at[i - 1], row, b)

    def forward_step(i):
        b = (z + i + (i == 1).astype(jnp.int32) - (i == 2).astype(jnp.int32)) % NZ
        row = group_row(s, z, b)

        @pl.when(i > 0)
        def _():
            remote(qh.at[b], qh.at[b], q_send.at[0], q_recv.at[b], row, b).wait_recv()
            transpose_heads(qh, qt, b)

        top[b] = score_block(s, z, b, kb, qt, scores)

        @pl.when(i == 0)
        def _():
            gather(vb, vt, v_pass, v_send, v_recv, pass_g)

        sums[b] = prob_block(s, z, b, top[b], vt, scores, probs, out_t)

    each(0, NZ, forward_step)

    def stats_step(i):
        b = (z + i + (i == 1).astype(jnp.int32) - (i == 2).astype(jnp.int32)) % NZ
        row = group_row(s, z, b)

        @pl.when(i > 0)
        def _():
            remote(gh.at[b], gh.at[b], g_send.at[0], g_recv.at[b], row, b).wait_recv()
            transpose_heads(gh, gt, b)

        stat_block(z, b, top[b], sums[b], gt, out_t, stats)
        each(1, NZ, lambda j: st_copy(b, j).start())

    each(0, NZ, stats_step)

    def send_o(i):
        b, row = member(i)
        o_out[b] = out_t[b].astype(BF16)
        o_copy(i).start()

    each(1, NZ, send_o)

    def merge(b, parts=None):
        def wait(j):
            p, row = member(j)
            remote(
                stats.at[b, p], stats.at[b, p], st_send.at[b, 0], st_recv.at[b, p], row, p
            ).wait_recv()

        each(1, NZ, wait)
        merge_stats(b, stats, top, coef, delta, parts)

    def tile(b, c, size):
        backward_tile(s, z, b, c, size, vb, kt, qh, gh, gt, probs, coef, delta, dq_t, dkv)

    def send_dq(i):
        b = (z + i) % NZ
        dq_out[b] = dq_t[b].astype(BF16)
        dq_copy(i).start()

    for i in (1, 3):
        b = (z + i) % NZ
        merge(b)
        tiles(chunks_of(s, z, b), lambda c, size, now: (tile(b, c, size), now)[1], 0)
        send_dq(i)

    merge((z + 2) % NZ)
    merge(z, part_coef)

    def round_at(i):
        k = i % 4
        ny = (y // 2 + i + i // 4) % 2
        nx = (x + k + (k == 2).astype(jnp.int32) - (k == 3).astype(jnp.int32)) % 4
        return ny * 4 + nx

    def core_rows(i, which):
        return pl.ds(pl.multiple_of(round_at(i) * 4 * T + which * 2 * T, 2 * T), 2 * T)

    def sib_copy(i):
        return remote(
            dkv.at[core_rows(i, 1 - core), :], sib_in.at[i], sib_send.at[i], sib_recv.at[i], sibling, z
        )

    def dkv_copy(i, j):
        row = round_at(i) * 4 + core * 2 + j
        return remote(
            kv_out.at[2 * i + j], kv_in.at[chip], dkv_send.at[2 * i + j], dkv_recv.at[chip], row, z
        )

    def finish(i):
        sib_copy(i).wait_recv()
        for j in range(2):
            rows = pl.ds(pl.multiple_of(round_at(i) * 4 * T + core * 2 * T + j * T, T), T)
            terms = dkv[rows, :] + sib_in[i, pl.ds(j * T, T), :]
            kv_out[2 * i + j, pl.ds(0, T), :] = (terms[:, :D] * SCALE).astype(BF16)
            kv_out[2 * i + j, pl.ds(T, T), :] = terms[:, D:].astype(BF16)
            mine = (i == 0) & (y % 2 == j)

            @pl.when(jnp.logical_not(mine))
            def _():
                dkv_copy(i, j).start()

            @pl.when(mine)
            def _():
                kv_in[chip] = kv_out[2 * i + j]

    def round_step(i):
        c = 2 * round_at(i)

        def one(j):
            b = (z + 2 * j) % NZ
            left = chunks_of(s, z, b) - c

            @pl.when(left > 1)
            def _():
                tile(b, c, 2)

            @pl.when(left == 1)
            def _():
                tile(b, c, 1)

        each(0, 2, one)
        sib_copy(i).start()

        @pl.when(i > 1)
        def _():
            finish(i - 2)

    each(0, ROUNDS, round_step)
    send_dq(2)
    each(ROUNDS - 2, ROUNDS, finish)

    for i in range(1, NZ):
        o_copy(i).wait_recv()
    out_t[z] = out_t[z] * coef[z] + sum(
        o_in[i - 1].astype(F32) * part_coef[(z - i + NZ) % NZ] for i in range(1, NZ)
    )
    for h in range(HEADS):
        att_ref[:, pl.ds(h * D, D)] = out_t[z, :, pl.ds(h * T, T)].T.astype(BF16)

    for i in range(1, NZ):
        dq_copy(i).wait_recv()
    dq_t[z] = (dq_t[z] + sum(dq_in[i].astype(F32) for i in range(NZ - 1))) * SCALE
    for h in range(HEADS):
        gq_ref[:, pl.ds(h * D, D)] = dq_t[z, :, pl.ds(h * T, T)].T.astype(BF16)

    def wait_kv(i):
        row = (i // 2) * 4 + core * 2 + i % 2

        @pl.when(i != chip)
        def _():
            remote(kv_out.at[0], kv_in.at[i], dkv_send.at[0], dkv_recv.at[i], row, z).wait_recv()

    each(0, NS // 2, wait_kv)
    for part in range(4):
        rows = pl.ds(part * T // 4, T // 4)
        gk_ref[rows, :] = jnp.sum(kv_in[:, rows, :].astype(F32), axis=0).astype(BF16)
        rows = pl.ds(T + part * T // 4, T // 4)
        gv_ref[pl.ds(part * T // 4, T // 4), :] = jnp.sum(kv_in[:, rows, :].astype(F32), axis=0).astype(BF16)

    each(1, NS // 2, lambda i: k_copy(i).wait_send())
    each(1, NS // 2, lambda i: v_copy(i).wait_send())
    each(0, NS // 2, lambda i: k_pass(i).wait_send())
    each(0, NS // 2, lambda i: v_pass(i).wait_send())

    for i in range(2):
        q_copy(i).wait_send()
        g_copy(i).wait_send()
        q_pass(i).wait_send()
        g_pass(i).wait_send()
    for i in range(1, NZ):
        o_copy(i).wait_send()
        dq_copy(i).wait_send()
    each(0, NZ, lambda b: each(1, NZ, lambda j: st_copy(b, j).wait_send()))

    def drain_kv(i):
        sib_copy(i).wait_send()
        for j in range(2):

            @pl.when((i != 0) | (y % 2 != j))
            def _():
                dkv_copy(i, j).wait_send()

    each(0, ROUNDS, drain_kv)


def hand_on(*refs):
    for i in range(4):
        refs[4 + i][...] = refs[i][...]


def shards(queries, keys, values, grad_out):
    vmem = pl.BlockSpec(memory_space=pltpu.VMEM)
    dma = pltpu.SemaphoreType.DMA
    results = pl.pallas_call(
        kernel,
        out_shape=(
            jax.ShapeDtypeStruct((T, QC), BF16),
            jax.ShapeDtypeStruct((T, QC), BF16),
            jax.ShapeDtypeStruct((T, D), BF16),
            jax.ShapeDtypeStruct((T, D), BF16),
        ),
        in_specs=[vmem] * 4,
        out_specs=(vmem,) * 4,
        scratch_shapes=[
            pltpu.VMEM((NS, T, D), BF16),
            pltpu.VMEM((NS, T, D), BF16),
            pltpu.VMEM((D, NS * T), BF16),
            pltpu.VMEM((D, NS * T), BF16),
            pltpu.VMEM((NZ, QC, D), BF16),
            pltpu.VMEM((NZ, QC, D), BF16),
            pltpu.VMEM((NZ, D, QC), BF16),
            pltpu.VMEM((NZ, D, QC), BF16),
            pltpu.VMEM((NCH, CK, QC), F32),
            pltpu.VMEM((MAXP, CK, QC), BF16),
            pltpu.VMEM((NZ, D, QC), F32),
            pltpu.VMEM((NZ, D, QC), F32),
            pltpu.VMEM((NZ, NZ, 24, T), F32),
            pltpu.VMEM((NZ, 1, QC), F32),
            pltpu.VMEM((NZ, 1, QC), F32),
            pltpu.VMEM((NZ, 1, QC), F32),
            pltpu.VMEM((NZ, 1, QC), F32),
            pltpu.VMEM((NS * T, 2 * D), F32),
            pltpu.VMEM((ROUNDS, 2 * T, 2 * D), F32),
            pltpu.VMEM((NCH, 2 * T, D), BF16),
            pltpu.VMEM((NS // 2, 2 * T, D), BF16),
            pltpu.VMEM((QC, D), BF16),
            pltpu.VMEM((QC, D), BF16),
            pltpu.VMEM((NZ, D, QC), BF16),
            pltpu.VMEM((NZ - 1, D, QC), BF16),
            pltpu.VMEM((NZ, 1, QC), F32),
            pltpu.VMEM((NZ, D, QC), BF16),
            pltpu.VMEM((NZ - 1, D, QC), BF16),
            dma((NS // 2,)),
            dma((NS,)),
            dma((NS // 2,)),
            dma((NS // 2,)),
            dma((NS,)),
            dma((NS // 2,)),
            dma((2,)),
            dma((NZ,)),
            dma(()),
            dma((2,)),
            dma((2,)),
            dma((NZ,)),
            dma(()),
            dma((2,)),
            dma((NZ, NZ)),
            dma((NZ, NZ)),
            dma((NZ,)),
            dma((NZ - 1,)),
            dma((NZ,)),
            dma((NZ - 1,)),
            dma((ROUNDS,)),
            dma((ROUNDS,)),
            dma((NCH,)),
            dma((NS // 2,)),
        ],
        compiler_params=pltpu.CompilerParams(
            collective_id=0, has_side_effects=True, vmem_limit_bytes=60 * 1024 * 1024
        ),
        cost_estimate=pl.CostEstimate(
            flops=10_000_000_000, bytes_accessed=10_000_000, transcendentals=6_500_000
        ),
    )(queries, keys, values, grad_out)
    return pl.pallas_call(
        hand_on,
        out_shape=tuple(jax.ShapeDtypeStruct(r.shape, r.dtype) for r in results),
        in_specs=[vmem] * 4,
        out_specs=(vmem,) * 4,
    )(*results)


def solution(mesh):
    spec = P(("ctxa", "ctxb"), None)
    return jax.shard_map(
        shards,
        mesh=mesh,
        in_specs=(spec,) * 4,
        out_specs=(spec,) * 4,
        check_vma=False,
    )
```

```python
import functools
import math

import jax
import jax.numpy as jnp
from jax import lax
from jax.experimental import pallas as pl
from jax.experimental.pallas import tpu as pltpu
from jax.sharding import PartitionSpec as P

MESH = pl.DeviceIdType.MESH
BF16 = jnp.bfloat16
F32 = jnp.float32

HEADS = 6
D = 128
T = 128
QC = HEADS * T
NS = 32
NZ = 4
CB = 2
CK = CB * T
NCH = NS // CB
ROUNDS = NS // 4
MAXP = 36
SCALE = D ** -0.5
C2 = SCALE * math.log2(math.e)
LOW = -1e30


def group_row(s, z, b):
    flip = (b + z) % 2
    return s + flip * (NS - 1 - 2 * s)


def chunks_of(s, z, b):
    seen = group_row(s, z, b) + (b >= z).astype(jnp.int32)
    return (seen + CB - 1) // CB


def base_of(s, z, b):
    total = jnp.int32(0)
    for other in range(NZ):
        total = total + jnp.where(other < b, chunks_of(s, z, jnp.int32(other)), 0)
    return total


def transpose_heads(src, dst, b):
    for h in range(HEADS):
        dst[b, :, pl.ds(h * T, T)] = src[b, pl.ds(h * T, T), :].T


def transpose_rows(src, dst, row):
    dst[:, pl.ds(pl.multiple_of(row * T, T), T)] = src[row].T


def rows_of(src, c, size):
    return src[pl.ds(c * CB, size * CB)].reshape(size * CK, D)


def lanes_of(src, c, size):
    return src[:, pl.ds(pl.multiple_of(c * CK, CK), size * CK)]


def tiles(count, step, carry):
    big = count // 4
    carry = lax.fori_loop(0, big, lambda i, now: step(4 * i, 4, now), carry)
    carry = lax.fori_loop(0, (count % 4) // 2, lambda i, now: step(4 * big, 2, now), carry)
    return lax.fori_loop(0, count % 2, lambda i, now: step(count - 1, 1, now), carry)


def score_block(s, z, b, kb, qt, scores):
    count = chunks_of(s, z, b)
    q_block = group_row(s, z, b) * NZ + b

    def keep(c, size, high, x):
        scores[pl.ds(c, size)] = x.reshape(size, CK, QC)
        return jnp.maximum(high, jnp.max(x.reshape(size * CK // 8, 8, QC), axis=0))

    def score(c, size):
        return jnp.dot(rows_of(kb, c, size), qt[b], preferred_element_type=F32)

    def plain(c, size, high):
        return keep(c, size, high, score(c, size))

    def masked(c, size, high):
        row = lax.broadcasted_iota(jnp.int32, (size * CK, QC), 0)
        col = lax.broadcasted_iota(jnp.int32, (size * CK, QC), 1)
        key_pos = ((c * CB + row // T) * NZ + z) * T + row % T
        q_pos = q_block * T + col % T
        return keep(c, size, high, jnp.where(key_pos <= q_pos, score(c, size), LOW))

    odd = count % 2
    even = ((count > 0) & (odd == 0)).astype(jnp.int32)
    high = jnp.full((8, QC), LOW, F32)
    high = tiles(count - odd - 2 * even, plain, high)
    high = lax.fori_loop(0, even, lambda i, now: masked(count - 2, 2, now), high)
    high = lax.fori_loop(0, odd, lambda i, now: masked(count - 1, 1, now), high)
    return jnp.max(high, axis=0, keepdims=True) * C2


def prob_block(s, z, b, row_max, vt, scores, probs, out_t):
    base = base_of(s, z, b)
    out_t[b] = jnp.zeros((D, QC), F32)

    def step(c, size, total):
        p = jnp.exp2(scores[pl.ds(c, size)].reshape(size * CK, QC) * C2 - row_max)
        total = total + jnp.sum(p.reshape(size * CK // 8, 8, QC), axis=0)
        pb = p.astype(BF16)
        probs[pl.ds(base + c, size)] = pb.reshape(size, CK, QC)
        out_t[b] += jnp.dot(lanes_of(vt, c, size), pb, preferred_element_type=F32)
        return total

    total = tiles(chunks_of(s, z, b), step, jnp.zeros((8, QC), F32))
    return jnp.sum(total, axis=0, keepdims=True)


def by_head(row):
    parts = [row[:, h * T : (h + 1) * T] for h in range(HEADS)]
    return jnp.concatenate(parts + [jnp.zeros((8 - HEADS, T), F32)], axis=0)


def in_line(rows):
    return jnp.concatenate([rows[h : h + 1] for h in range(HEADS)], axis=1)


def stat_block(z, b, row_max, row_sum, gt, out_t, stats):
    part_delta = jnp.sum(gt[b].astype(F32) * out_t[b], axis=0, keepdims=True)
    row_sum = jnp.maximum(row_sum, 1e-37)
    stats[b, z, pl.ds(0, 8), :] = by_head(row_max + jnp.log2(row_sum))
    stats[b, z, pl.ds(8, 8), :] = by_head(part_delta / row_sum)
    stats[b, z, pl.ds(16, 8), :] = by_head(row_max)


def merge_stats(b, stats, top, coef, delta, parts):
    logs = [stats[b, j, pl.ds(0, 8), :] for j in range(NZ)]
    high = functools.reduce(jnp.maximum, logs)
    log_total = high + jnp.log2(sum(jnp.exp2(x - high) for x in logs))
    shares = [jnp.exp2(x - log_total) for x in logs]
    coef[b] = jnp.exp2(top[b] - in_line(log_total))
    if parts is not None:
        for j in range(NZ):
            parts[j] = in_line(jnp.exp2(stats[b, j, pl.ds(16, 8), :] - log_total))
    delta[b] = in_line(sum(stats[b, j, pl.ds(8, 8), :] * shares[j] for j in range(NZ)))


def backward_tile(s, z, blocks, c, size, vb, kt, qh, gh, gt, probs, coef, delta, dq_t, dkv):
    key_sum, value_sum = 0.0, 0.0
    for b in blocks:
        base = base_of(s, z, b)
        dw = jnp.dot(rows_of(vb, c, size), gt[b], preferred_element_type=F32)
        w = probs[pl.ds(base + c, size)].reshape(size * CK, QC).astype(F32) * coef[b]
        ds = (w * (dw - delta[b])).astype(BF16)
        key_sum += jnp.dot(ds, qh[b], preferred_element_type=F32)
        value_sum += jnp.dot(w.astype(BF16), gh[b], preferred_element_type=F32)
        dq_t[b] += jnp.dot(lanes_of(kt, c, size), ds, preferred_element_type=F32)
    rows = pl.ds(pl.multiple_of(c * CK, CK), size * CK)
    dkv[rows, pl.ds(0, D)] += key_sum
    dkv[rows, pl.ds(D, D)] += value_sum


def kernel(
    q_ref, k_ref, v_ref, g_ref,
    att_ref, gq_ref, gk_ref, gv_ref,
    kb, vb, kt, vt, qh, gh, qt, gt, scores, probs, out_t, dq_t, stats, top, sums, coef, delta, dkv,
    sib_in, kv_out, kv_in, q_mid, g_mid, o_out, o_in, part_coef, dq_out, dq_in,
    k_send, k_recv, kf_send, v_send, v_recv, vf_send, q_send, q_recv, qm_recv, qp_send, g_send, g_recv, gm_recv, gp_send,
    st_send, st_recv, o_send, o_recv, dq_send, dq_recv, sib_send, sib_recv, dkv_send, dkv_recv, load_sem, store_sem,
    att_rows, gq_rows, gk_rows, gv_rows,
):
    ia = lax.axis_index("ctxa")
    ib = lax.axis_index("ctxb")
    z = ib % NZ
    s = ia * 2 + ib // NZ
    core = ia % 2
    x = (ia // 2) % 4
    y = (ia // 8) * 2 + ib // NZ
    sibling = s + 2 - 4 * core
    mirror = NS - 1 - s
    chip = (s // 4) * 2 + s % 2

    def device(row, plane):
        return (row // 2, (row % 2) * NZ + plane)

    def remote(src, dst, send, recv, row, plane):
        return pltpu.make_async_remote_copy(
            src_ref=src, dst_ref=dst, send_sem=send, recv_sem=recv,
            device_id=device(row, plane), device_id_type=MESH,
        )

    def each(low, high, step):
        lax.fori_loop(low, high, lambda i, _: (step(i), 0)[1], 0)

    def moved(i, sign):
        nx = (x + sign * (i % 4) + 4) % 4
        ny = (y + sign * (i // 4) + 4) % 4
        return (ny // 2) * 16 + nx * 4 + core * 2 + ny % 2

    def member(i):
        b = (z + i) % NZ
        return b, group_row(s, z, b)

    barrier = pltpu.get_barrier_semaphore()

    def signal(row, plane):
        pl.semaphore_signal(
            barrier, inc=1, device_id=device(row, plane), device_id_type=MESH
        )

    each(1, NS // 2, lambda i: signal(moved(i, 1), z))
    signal(sibling, z)
    for i in range(1, NZ):
        b, row = member(i)
        signal(row, b)
    signal(mirror, z)
    signal(s, (z + 1) % NZ)
    signal(s, (z + 3) % NZ)

    loads = [
        pltpu.make_async_copy(k_ref, kb.at[s], load_sem.at[0]),
        pltpu.make_async_copy(v_ref, vb.at[s], load_sem.at[1]),
    ]
    for h in range(HEADS):
        lanes, rows = pl.ds(h * D, D), pl.ds(h * T, T)
        loads.append(pltpu.make_async_copy(q_ref.at[:, lanes], qh.at[z, rows, :], load_sem.at[2 + h]))
        loads.append(
            pltpu.make_async_copy(g_ref.at[:, lanes], gh.at[z, rows, :], load_sem.at[2 + HEADS + h])
        )
    for load in loads:
        load.start()
    for load in loads:
        load.wait()

    pl.semaphore_wait(barrier, NS // 2 - 1 + 1 + NZ - 1 + 3)

    def k_copy(i):
        return remote(kb.at[s], kb.at[s], k_send.at[i], k_recv.at[s], moved(i, 1), z)

    def v_copy(i):
        return remote(vb.at[s], vb.at[s], v_send.at[i], v_recv.at[s], moved(i, 1), z)

    def q_copy(i):
        if i == 0:
            return remote(qh.at[z], q_mid, q_send.at[0], qm_recv, mirror, z)
        return remote(qh.at[z], qh.at[z], q_send.at[1], q_recv.at[z], s, (z + 2) % NZ)

    def g_copy(i):
        if i == 0:
            return remote(gh.at[z], g_mid, g_send.at[0], gm_recv, mirror, z)
        return remote(gh.at[z], gh.at[z], g_send.at[1], g_recv.at[z], s, (z + 2) % NZ)

    def q_pass(i):
        return remote(q_mid, qh.at[z], qp_send.at[i], q_recv.at[z], s, (z + 1 + 2 * i) % NZ)

    def g_pass(i):
        return remote(g_mid, gh.at[z], gp_send.at[i], g_recv.at[z], s, (z + 1 + 2 * i) % NZ)

    def k_pass(i):
        row = moved(i, -1)
        return remote(kb.at[row], kb.at[row], kf_send.at[i], k_recv.at[row], sibling, z)

    def v_pass(i):
        row = moved(i, -1)
        return remote(vb.at[row], vb.at[row], vf_send.at[i], v_recv.at[row], sibling, z)

    q_copy(0).start()
    q_copy(1).start()
    each(1, NS // 2, lambda i: k_copy(i).start())
    each(1, NS // 2, lambda i: v_copy(i).start())
    g_copy(0).start()
    g_copy(1).start()

    transpose_heads(qh, qt, z)
    transpose_heads(gh, gt, z)
    dkv[...] = jnp.zeros((NS * T, 2 * D), F32)
    dq_t[...] = jnp.zeros((NZ, D, QC), F32)

    def gather(buf, flipped, copy, send, recv, between):
        def wait(row):
            remote(buf.at[row], buf.at[row], send.at[0], recv.at[row], sibling, z).wait_recv()

        def near(i):
            row = moved(i, -1)

            @pl.when(i > 0)
            def _():
                wait(row)

            copy(i).start()
            transpose_rows(buf, flipped, row)

        def far(i):
            row = moved(i, -1) + 2 - 4 * core
            wait(row)
            transpose_rows(buf, flipped, row)

        each(0, NS // 2, near)
        between()
        each(0, NS // 2, far)

    def pass_q():
        q_copy(0).wait_recv()
        q_pass(0).start()
        q_pass(1).start()

    def pass_g():
        g_copy(0).wait_recv()
        g_pass(0).start()
        g_pass(1).start()

    gather(kb, kt, k_pass, k_send, k_recv, pass_q)

    def st_copy(b, i):
        p, row = member(i)
        return remote(stats.at[b, z], stats.at[b, z], st_send.at[b, i], st_recv.at[b, z], row, p)

    def o_copy(i):
        b, row = member(i)
        return remote(o_out.at[b], o_in.at[i - 1], o_send.at[i], o_recv.at[i - 1], row, b)

    def dq_copy(i):
        b, row = member(i)
        return remote(dq_out.at[b], dq_in.at[i - 1], dq_send.at[i], dq_recv.at[i - 1], row, b)

    def forward_step(i):
        b = (z + i + (i == 1).astype(jnp.int32) - (i == 2).astype(jnp.int32)) % NZ
        row = group_row(s, z, b)

        @pl.when(i > 0)
        def _():
            remote(qh.at[b], qh.at[b], q_send.at[0], q_recv.at[b], row, b).wait_recv()
            transpose_heads(qh, qt, b)

        top[b] = score_block(s, z, b, kb, qt, scores)

        @pl.when(i == 0)
        def _():
            gather(vb, vt, v_pass, v_send, v_recv, pass_g)

        sums[b] = prob_block(s, z, b, top[b], vt, scores, probs, out_t)

    each(0, NZ, forward_step)

    def stats_step(i):
        b = (z + i + (i == 1).astype(jnp.int32) - (i == 2).astype(jnp.int32)) % NZ
        row = group_row(s, z, b)

        @pl.when(i > 0)
        def _():
            remote(gh.at[b], gh.at[b], g_send.at[0], g_recv.at[b], row, b).wait_recv()
            transpose_heads(gh, gt, b)

        stat_block(z, b, top[b], sums[b], gt, out_t, stats)
        each(1, NZ, lambda j: st_copy(b, j).start())

    each(0, NZ, stats_step)

    def send_o(i):
        b, row = member(i)
        o_out[b] = out_t[b].astype(BF16)
        o_copy(i).start()

    each(1, NZ, send_o)

    def merge(b, parts=None):
        def wait(j):
            p, row = member(j)
            remote(
                stats.at[b, p], stats.at[b, p], st_send.at[b, 0], st_recv.at[b, p], row, p
            ).wait_recv()

        each(1, NZ, wait)
        merge_stats(b, stats, top, coef, delta, parts)

    def tile(blocks, c, size):
        backward_tile(s, z, blocks, c, size, vb, kt, qh, gh, gt, probs, coef, delta, dq_t, dkv)

    def send_dq(i):
        b = (z + i) % NZ
        dq_out[b] = dq_t[b].astype(BF16)
        dq_copy(i).start()

    for i in (1, 3):
        b = (z + i) % NZ
        merge(b)
        tiles(chunks_of(s, z, b), lambda c, size, now: (tile((b,), c, size), now)[1], 0)
        send_dq(i)

    merge((z + 2) % NZ)
    merge(z, part_coef)

    def round_at(i):
        k = i % 4
        ny = (y // 2 + i + i // 4) % 2
        nx = (x + k + (k == 2).astype(jnp.int32) - (k == 3).astype(jnp.int32)) % 4
        return ny * 4 + nx

    def core_rows(i, which):
        return pl.ds(pl.multiple_of(round_at(i) * 4 * T + which * 2 * T, 2 * T), 2 * T)

    def sib_copy(i):
        return remote(
            dkv.at[core_rows(i, 1 - core), :], sib_in.at[i], sib_send.at[i], sib_recv.at[i], sibling, z
        )

    def dkv_copy(i, j):
        row = round_at(i) * 4 + core * 2 + j
        return remote(
            kv_out.at[2 * i + j], kv_in.at[chip], dkv_send.at[2 * i + j], dkv_recv.at[chip], row, z
        )

    def finish(i):
        sib_copy(i).wait_recv()
        for j in range(2):
            rows = pl.ds(pl.multiple_of(round_at(i) * 4 * T + core * 2 * T + j * T, T), T)
            terms = dkv[rows, :] + sib_in[i, pl.ds(j * T, T), :]
            kv_out[2 * i + j, pl.ds(0, T), :] = (terms[:, :D] * SCALE).astype(BF16)
            kv_out[2 * i + j, pl.ds(T, T), :] = terms[:, D:].astype(BF16)
            mine = (i == 0) & (y % 2 == j)

            @pl.when(jnp.logical_not(mine))
            def _():
                dkv_copy(i, j).start()

            @pl.when(mine)
            def _():
                kv_in[chip] = kv_out[2 * i + j]

    def round_step(i):
        c = 2 * round_at(i)

        pair = (z, (z + 2) % NZ)
        left = [chunks_of(s, z, b) - c for b in pair]
        whole = (left[0] > 1) & (left[1] > 1)

        @pl.when(whole)
        def _():
            tile(pair, c, 2)

        def one(j):
            b = (z + 2 * j) % NZ
            rest = chunks_of(s, z, b) - c

            @pl.when((rest > 1) & jnp.logical_not(whole))
            def _():
                tile((b,), c, 2)

            @pl.when(rest == 1)
            def _():
                tile((b,), c, 1)

        each(0, 2, one)
        sib_copy(i).start()

        @pl.when(i > 1)
        def _():
            finish(i - 2)

    each(0, ROUNDS, round_step)
    send_dq(2)
    each(ROUNDS - 2, ROUNDS, finish)

    for i in range(1, NZ):
        o_copy(i).wait_recv()
    out_t[z] = out_t[z] * coef[z] + sum(
        o_in[i - 1].astype(F32) * part_coef[(z - i + NZ) % NZ] for i in range(1, NZ)
    )
    for h in range(HEADS):
        att_rows[:, pl.ds(h * D, D)] = out_t[z, :, pl.ds(h * T, T)].T.astype(BF16)
    att_store = pltpu.make_async_copy(att_rows, att_ref, store_sem.at[0])
    att_store.start()

    each(1, NS // 2, lambda i: k_copy(i).wait_send())
    each(1, NS // 2, lambda i: v_copy(i).wait_send())
    each(0, NS // 2, lambda i: k_pass(i).wait_send())
    each(0, NS // 2, lambda i: v_pass(i).wait_send())

    for i in range(2):
        q_copy(i).wait_send()
        g_copy(i).wait_send()
        q_pass(i).wait_send()
        g_pass(i).wait_send()
    for i in range(1, NZ):
        o_copy(i).wait_send()
    each(0, NZ, lambda b: each(1, NZ, lambda j: st_copy(b, j).wait_send()))


    for i in range(1, NZ):
        dq_copy(i).wait_recv()
    dq_t[z] = (dq_t[z] + sum(dq_in[i].astype(F32) for i in range(NZ - 1))) * SCALE
    for h in range(HEADS):
        gq_rows[:, pl.ds(h * D, D)] = dq_t[z, :, pl.ds(h * T, T)].T.astype(BF16)
    gq_store = pltpu.make_async_copy(gq_rows, gq_ref, store_sem.at[1])
    gq_store.start()

    def drain_kv(i):
        sib_copy(i).wait_send()
        for j in range(2):

            @pl.when((i != 0) | (y % 2 != j))
            def _():
                dkv_copy(i, j).wait_send()

    each(0, ROUNDS, drain_kv)
    for i in range(1, NZ):
        dq_copy(i).wait_send()

    def wait_kv(i):
        row = (i // 2) * 4 + core * 2 + i % 2

        @pl.when(i != chip)
        def _():
            remote(kv_out.at[0], kv_in.at[i], dkv_send.at[0], dkv_recv.at[i], row, z).wait_recv()

    each(0, NS // 2, wait_kv)
    for part in range(4):
        rows = pl.ds(part * T // 4, T // 4)
        gk_rows[rows, :] = jnp.sum(kv_in[:, rows, :].astype(F32), axis=0).astype(BF16)
        rows = pl.ds(T + part * T // 4, T // 4)
        gv_rows[pl.ds(part * T // 4, T // 4), :] = jnp.sum(kv_in[:, rows, :].astype(F32), axis=0).astype(BF16)
    gk_store = pltpu.make_async_copy(gk_rows, gk_ref, store_sem.at[2])
    gv_store = pltpu.make_async_copy(gv_rows, gv_ref, store_sem.at[3])
    gk_store.start()
    gv_store.start()
    att_store.wait()
    gq_store.wait()
    gk_store.wait()
    gv_store.wait()


def hand_on(*refs):
    for i in range(4):
        refs[4 + i][...] = refs[i][...]


def shards(queries, keys, values, grad_out):
    whole = pl.BlockSpec(memory_space=pl.ANY)
    vmem = pl.BlockSpec(memory_space=pltpu.VMEM)
    dma = pltpu.SemaphoreType.DMA
    results = pl.pallas_call(
        kernel,
        out_shape=(
            jax.ShapeDtypeStruct((T, QC), BF16),
            jax.ShapeDtypeStruct((T, QC), BF16),
            jax.ShapeDtypeStruct((T, D), BF16),
            jax.ShapeDtypeStruct((T, D), BF16),
        ),
        in_specs=[whole] * 4,
        out_specs=(whole,) * 4,
        scratch_shapes=[
            pltpu.VMEM((NS, T, D), BF16),
            pltpu.VMEM((NS, T, D), BF16),
            pltpu.VMEM((D, NS * T), BF16),
            pltpu.VMEM((D, NS * T), BF16),
            pltpu.VMEM((NZ, QC, D), BF16),
            pltpu.VMEM((NZ, QC, D), BF16),
            pltpu.VMEM((NZ, D, QC), BF16),
            pltpu.VMEM((NZ, D, QC), BF16),
            pltpu.VMEM((NCH, CK, QC), F32),
            pltpu.VMEM((MAXP, CK, QC), BF16),
            pltpu.VMEM((NZ, D, QC), F32),
            pltpu.VMEM((NZ, D, QC), F32),
            pltpu.VMEM((NZ, NZ, 24, T), F32),
            pltpu.VMEM((NZ, 1, QC), F32),
            pltpu.VMEM((NZ, 1, QC), F32),
            pltpu.VMEM((NZ, 1, QC), F32),
            pltpu.VMEM((NZ, 1, QC), F32),
            pltpu.VMEM((NS * T, 2 * D), F32),
            pltpu.VMEM((ROUNDS, 2 * T, 2 * D), F32),
            pltpu.VMEM((NCH, 2 * T, D), BF16),
            pltpu.VMEM((NS // 2, 2 * T, D), BF16),
            pltpu.VMEM((QC, D), BF16),
            pltpu.VMEM((QC, D), BF16),
            pltpu.VMEM((NZ, D, QC), BF16),
            pltpu.VMEM((NZ - 1, D, QC), BF16),
            pltpu.VMEM((NZ, 1, QC), F32),
            pltpu.VMEM((NZ, D, QC), BF16),
            pltpu.VMEM((NZ - 1, D, QC), BF16),
            dma((NS // 2,)),
            dma((NS,)),
            dma((NS // 2,)),
            dma((NS // 2,)),
            dma((NS,)),
            dma((NS // 2,)),
            dma((2,)),
            dma((NZ,)),
            dma(()),
            dma((2,)),
            dma((2,)),
            dma((NZ,)),
            dma(()),
            dma((2,)),
            dma((NZ, NZ)),
            dma((NZ, NZ)),
            dma((NZ,)),
            dma((NZ - 1,)),
            dma((NZ,)),
            dma((NZ - 1,)),
            dma((ROUNDS,)),
            dma((ROUNDS,)),
            dma((NCH,)),
            dma((NS // 2,)),
            dma((2 + 2 * HEADS,)),
            dma((4,)),
            pltpu.VMEM((T, QC), BF16),
            pltpu.VMEM((T, QC), BF16),
            pltpu.VMEM((T, D), BF16),
            pltpu.VMEM((T, D), BF16),
        ],
        compiler_params=pltpu.CompilerParams(
            collective_id=0, has_side_effects=True, vmem_limit_bytes=60 * 1024 * 1024
        ),
        cost_estimate=pl.CostEstimate(
            flops=10_000_000_000, bytes_accessed=10_000_000, transcendentals=6_500_000
        ),
    )(queries, keys, values, grad_out)
    return pl.pallas_call(
        hand_on,
        out_shape=tuple(jax.ShapeDtypeStruct(r.shape, r.dtype) for r in results),
        in_specs=[vmem] * 4,
        out_specs=(vmem,) * 4,
    )(*results)


def solution(mesh):
    spec = P(("ctxa", "ctxb"), None)
    return jax.shard_map(
        shards,
        mesh=mesh,
        in_specs=(spec,) * 4,
        out_specs=(spec,) * 4,
        check_vma=False,
    )
```

```python
import functools
import math

import jax
import jax.numpy as jnp
from jax import lax
from jax.experimental import pallas as pl
from jax.experimental.pallas import tpu as pltpu
from jax.sharding import PartitionSpec as P

MESH = pl.DeviceIdType.MESH
BF16 = jnp.bfloat16
F32 = jnp.float32

HEADS = 6
D = 128
T = 128
QC = HEADS * T
NS = 32
NZ = 4
CB = 2
CK = CB * T
NCH = NS // CB
ROUNDS = NS // 4
MAXP = 36
SCALE = D ** -0.5
C2 = SCALE * math.log2(math.e)
LOW = -1e30


def group_row(s, z, b):
    flip = (b + z) % 2
    return s + flip * (NS - 1 - 2 * s)


def chunks_of(s, z, b):
    seen = group_row(s, z, b) + (b >= z).astype(jnp.int32)
    return (seen + CB - 1) // CB


def base_of(s, z, b):
    total = jnp.int32(0)
    for other in range(NZ):
        total = total + jnp.where(other < b, chunks_of(s, z, jnp.int32(other)), 0)
    return total


def transpose_heads(src, dst, b):
    for h in range(HEADS):
        dst[b, :, pl.ds(h * T, T)] = src[b, pl.ds(h * T, T), :].T


def transpose_rows(src, dst, row):
    dst[:, pl.ds(pl.multiple_of(row * T, T), T)] = src[row].T


def rows_of(src, c, size):
    return src[pl.ds(c * CB, size * CB)].reshape(size * CK, D)


def lanes_of(src, c, size):
    return src[:, pl.ds(pl.multiple_of(c * CK, CK), size * CK)]


def tiles(count, step, carry):
    big = count // 4
    carry = lax.fori_loop(0, big, lambda i, now: step(4 * i, 4, now), carry)
    carry = lax.fori_loop(0, (count % 4) // 2, lambda i, now: step(4 * big, 2, now), carry)
    return lax.fori_loop(0, count % 2, lambda i, now: step(count - 1, 1, now), carry)


def score_block(s, z, b, kb, qt, scores):
    count = chunks_of(s, z, b)
    q_block = group_row(s, z, b) * NZ + b

    def keep(c, size, high, x):
        scores[pl.ds(c, size)] = x.reshape(size, CK, QC)
        return jnp.maximum(high, jnp.max(x.reshape(size * CK // 8, 8, QC), axis=0))

    def score(c, size):
        return jnp.dot(rows_of(kb, c, size), qt[b], preferred_element_type=F32)

    def plain(c, size, high):
        return keep(c, size, high, score(c, size))

    def masked(c, size, high):
        row = lax.broadcasted_iota(jnp.int32, (size * CK, QC), 0)
        col = lax.broadcasted_iota(jnp.int32, (size * CK, QC), 1)
        key_pos = ((c * CB + row // T) * NZ + z) * T + row % T
        q_pos = q_block * T + col % T
        return keep(c, size, high, jnp.where(key_pos <= q_pos, score(c, size), LOW))

    odd = count % 2
    even = ((count > 0) & (odd == 0)).astype(jnp.int32)
    high = jnp.full((8, QC), LOW, F32)
    high = tiles(count - odd - 2 * even, plain, high)
    high = lax.fori_loop(0, even, lambda i, now: masked(count - 2, 2, now), high)
    high = lax.fori_loop(0, odd, lambda i, now: masked(count - 1, 1, now), high)
    return jnp.max(high, axis=0, keepdims=True) * C2


def prob_block(s, z, b, row_max, vt, scores, probs, out_t):
    base = base_of(s, z, b)
    out_t[b] = jnp.zeros((D, QC), F32)

    def step(c, size, total):
        p = jnp.exp2(scores[pl.ds(c, size)].reshape(size * CK, QC) * C2 - row_max)
        total = total + jnp.sum(p.reshape(size * CK // 8, 8, QC), axis=0)
        pb = p.astype(BF16)
        probs[pl.ds(base + c, size)] = pb.reshape(size, CK, QC)
        out_t[b] += jnp.dot(lanes_of(vt, c, size), pb, preferred_element_type=F32)
        return total

    total = tiles(chunks_of(s, z, b), step, jnp.zeros((8, QC), F32))
    return jnp.sum(total, axis=0, keepdims=True)


def by_head(row):
    parts = [row[:, h * T : (h + 1) * T] for h in range(HEADS)]
    return jnp.concatenate(parts + [jnp.zeros((8 - HEADS, T), F32)], axis=0)


def in_line(rows):
    return jnp.concatenate([rows[h : h + 1] for h in range(HEADS)], axis=1)


def stat_block(z, b, row_max, row_sum, gt, out_t, stats):
    part_delta = jnp.sum(gt[b].astype(F32) * out_t[b], axis=0, keepdims=True)
    row_sum = jnp.maximum(row_sum, 1e-37)
    stats[b, z, pl.ds(0, 8), :] = by_head(row_max + jnp.log2(row_sum))
    stats[b, z, pl.ds(8, 8), :] = by_head(part_delta / row_sum)
    stats[b, z, pl.ds(16, 8), :] = by_head(row_max)


def merge_stats(b, stats, top, coef, delta, parts):
    logs = [stats[b, j, pl.ds(0, 8), :] for j in range(NZ)]
    high = functools.reduce(jnp.maximum, logs)
    log_total = high + jnp.log2(sum(jnp.exp2(x - high) for x in logs))
    shares = [jnp.exp2(x - log_total) for x in logs]
    coef[b] = jnp.exp2(top[b] - in_line(log_total))
    if parts is not None:
        for j in range(NZ):
            parts[j] = in_line(jnp.exp2(stats[b, j, pl.ds(16, 8), :] - log_total))
    delta[b] = in_line(sum(stats[b, j, pl.ds(8, 8), :] * shares[j] for j in range(NZ)))


def backward_tile(s, z, blocks, c, size, vb, kt, qh, gh, gt, probs, coef, delta, dq_t, dkv):
    key_sum, value_sum = 0.0, 0.0
    for b in blocks:
        base = base_of(s, z, b)
        dw = jnp.dot(rows_of(vb, c, size), gt[b], preferred_element_type=F32)
        w = probs[pl.ds(base + c, size)].reshape(size * CK, QC).astype(F32) * coef[b]
        ds = (w * (dw - delta[b])).astype(BF16)
        key_sum += jnp.dot(ds, qh[b], preferred_element_type=F32)
        value_sum += jnp.dot(w.astype(BF16), gh[b], preferred_element_type=F32)
        dq_t[b] += jnp.dot(lanes_of(kt, c, size), ds, preferred_element_type=F32)
    rows = pl.ds(pl.multiple_of(c * CK, CK), size * CK)
    dkv[rows, pl.ds(0, D)] += key_sum
    dkv[rows, pl.ds(D, D)] += value_sum


def kernel(
    q_ref, k_ref, v_ref, g_ref,
    att_ref, gq_ref, gk_ref, gv_ref,
    kb, vb, kt, vt, qh, gh, qt, gt, scores, probs, out_t, dq_t, stats, top, sums, coef, delta, dkv,
    sib_in, kv_out, kv_in, q_mid, g_mid, o_out, o_in, part_coef, dq_out, dq_in,
    k_send, k_recv, kf_send, v_send, v_recv, vf_send, q_send, q_recv, qm_recv, qp_send, g_send, g_recv, gm_recv, gp_send,
    st_send, st_recv, o_send, o_recv, dq_send, dq_recv, sib_send, sib_recv, dkv_send, dkv_recv, load_sem, store_sem,
    att_rows, gq_rows, gk_rows, gv_rows,
):
    ia = lax.axis_index("ctxa")
    ib = lax.axis_index("ctxb")
    z = ib % NZ
    s = ia * 2 + ib // NZ
    core = ia % 2
    x = (ia // 2) % 4
    y = (ia // 8) * 2 + ib // NZ
    sibling = s + 2 - 4 * core
    mirror = NS - 1 - s
    chip = (s // 4) * 2 + s % 2

    def device(row, plane):
        return (row // 2, (row % 2) * NZ + plane)

    def remote(src, dst, send, recv, row, plane):
        return pltpu.make_async_remote_copy(
            src_ref=src, dst_ref=dst, send_sem=send, recv_sem=recv,
            device_id=device(row, plane), device_id_type=MESH,
        )

    def each(low, high, step):
        lax.fori_loop(low, high, lambda i, _: (step(i), 0)[1], 0)

    def moved(i, sign):
        nx = (x + sign * (i % 4) + 4) % 4
        ny = (y + sign * (i // 4) + 4) % 4
        return (ny // 2) * 16 + nx * 4 + core * 2 + ny % 2

    def member(i):
        b = (z + i) % NZ
        return b, group_row(s, z, b)

    barrier = pltpu.get_barrier_semaphore()

    def signal(row, plane):
        pl.semaphore_signal(
            barrier, inc=1, device_id=device(row, plane), device_id_type=MESH
        )

    each(1, NS // 2, lambda i: signal(moved(i, 1), z))
    signal(sibling, z)
    for i in range(1, NZ):
        b, row = member(i)
        signal(row, b)
    signal(mirror, z)
    signal(s, (z + 1) % NZ)
    signal(s, (z + 3) % NZ)

    loads = [
        pltpu.make_async_copy(k_ref, kb.at[s], load_sem.at[0]),
        pltpu.make_async_copy(v_ref, vb.at[s], load_sem.at[1]),
    ]
    for h in range(HEADS):
        lanes, rows = pl.ds(h * D, D), pl.ds(h * T, T)
        loads.append(pltpu.make_async_copy(q_ref.at[:, lanes], qh.at[z, rows, :], load_sem.at[2 + h]))
        loads.append(
            pltpu.make_async_copy(g_ref.at[:, lanes], gh.at[z, rows, :], load_sem.at[2 + HEADS + h])
        )
    for load in loads:
        load.start()
    for load in loads:
        load.wait()

    pl.semaphore_wait(barrier, NS // 2 - 1 + 1 + NZ - 1 + 3)

    def k_copy(i):
        return remote(kb.at[s], kb.at[s], k_send.at[i], k_recv.at[s], moved(i, 1), z)

    def v_copy(i):
        return remote(vb.at[s], vb.at[s], v_send.at[i], v_recv.at[s], moved(i, 1), z)

    def q_copy(i):
        if i == 0:
            return remote(qh.at[z], q_mid, q_send.at[0], qm_recv, mirror, z)
        return remote(qh.at[z], qh.at[z], q_send.at[1], q_recv.at[z], s, (z + 2) % NZ)

    def g_copy(i):
        if i == 0:
            return remote(gh.at[z], g_mid, g_send.at[0], gm_recv, mirror, z)
        return remote(gh.at[z], gh.at[z], g_send.at[1], g_recv.at[z], s, (z + 2) % NZ)

    def q_pass(i):
        return remote(q_mid, qh.at[z], qp_send.at[i], q_recv.at[z], s, (z + 1 + 2 * i) % NZ)

    def g_pass(i):
        return remote(g_mid, gh.at[z], gp_send.at[i], g_recv.at[z], s, (z + 1 + 2 * i) % NZ)

    def k_pass(i):
        row = moved(i, -1)
        return remote(kb.at[row], kb.at[row], kf_send.at[i], k_recv.at[row], sibling, z)

    def v_pass(i):
        row = moved(i, -1)
        return remote(vb.at[row], vb.at[row], vf_send.at[i], v_recv.at[row], sibling, z)

    q_copy(0).start()
    q_copy(1).start()
    each(1, NS // 2, lambda i: k_copy(i).start())
    each(1, NS // 2, lambda i: v_copy(i).start())
    g_copy(0).start()
    g_copy(1).start()

    transpose_heads(qh, qt, z)
    transpose_heads(gh, gt, z)
    dkv[...] = jnp.zeros((NS * T, 2 * D), F32)
    dq_t[...] = jnp.zeros((NZ, D, QC), F32)

    def gather(buf, flipped, copy, send, recv, between):
        def wait(row):
            remote(buf.at[row], buf.at[row], send.at[0], recv.at[row], sibling, z).wait_recv()

        def near(i):
            row = moved(i, -1)

            @pl.when(i > 0)
            def _():
                wait(row)

            copy(i).start()
            transpose_rows(buf, flipped, row)

        def far(i):
            row = moved(i, -1) + 2 - 4 * core
            wait(row)
            transpose_rows(buf, flipped, row)

        each(0, NS // 2, near)
        between()
        each(0, NS // 2, far)

    def pass_q():
        q_copy(0).wait_recv()
        q_pass(0).start()
        q_pass(1).start()

    def pass_g():
        g_copy(0).wait_recv()
        g_pass(0).start()
        g_pass(1).start()

    gather(kb, kt, k_pass, k_send, k_recv, pass_q)

    def st_copy(b, i):
        p, row = member(i)
        return remote(stats.at[b, z], stats.at[b, z], st_send.at[b, i], st_recv.at[b, z], row, p)

    def o_copy(i):
        b, row = member(i)
        return remote(o_out.at[b], o_in.at[i - 1], o_send.at[i], o_recv.at[i - 1], row, b)

    def dq_copy(i):
        b, row = member(i)
        return remote(dq_out.at[b], dq_in.at[i - 1], dq_send.at[i], dq_recv.at[i - 1], row, b)

    def send_o(i):
        b, row = member(i)
        o_out[b] = out_t[b].astype(BF16)
        o_copy(i).start()

    def forward_step(i):
        b = (z + i + (i == 1).astype(jnp.int32) - (i == 2).astype(jnp.int32)) % NZ
        row = group_row(s, z, b)

        @pl.when(i > 0)
        def _():
            remote(qh.at[b], qh.at[b], q_send.at[0], q_recv.at[b], row, b).wait_recv()
            transpose_heads(qh, qt, b)

        top[b] = score_block(s, z, b, kb, qt, scores)

        @pl.when(i == 0)
        def _():
            gather(vb, vt, v_pass, v_send, v_recv, pass_g)

        sums[b] = prob_block(s, z, b, top[b], vt, scores, probs, out_t)

        @pl.when(i > 0)
        def _():
            send_o((b - z + NZ) % NZ)

    each(0, NZ, forward_step)

    def stats_step(i):
        b = (z + i + (i == 1).astype(jnp.int32) - (i == 2).astype(jnp.int32)) % NZ
        row = group_row(s, z, b)

        @pl.when(i > 0)
        def _():
            remote(gh.at[b], gh.at[b], g_send.at[0], g_recv.at[b], row, b).wait_recv()
            transpose_heads(gh, gt, b)

        stat_block(z, b, top[b], sums[b], gt, out_t, stats)
        each(1, NZ, lambda j: st_copy(b, j).start())

    each(0, NZ, stats_step)

    def merge(b, parts=None):
        def wait(j):
            p, row = member(j)
            remote(
                stats.at[b, p], stats.at[b, p], st_send.at[b, 0], st_recv.at[b, p], row, p
            ).wait_recv()

        each(1, NZ, wait)
        merge_stats(b, stats, top, coef, delta, parts)

    def tile(blocks, c, size):
        backward_tile(s, z, blocks, c, size, vb, kt, qh, gh, gt, probs, coef, delta, dq_t, dkv)

    def send_dq(i):
        b = (z + i) % NZ
        dq_out[b] = dq_t[b].astype(BF16)
        dq_copy(i).start()

    for i in (1, 3):
        b = (z + i) % NZ
        merge(b)
        tiles(chunks_of(s, z, b), lambda c, size, now: (tile((b,), c, size), now)[1], 0)
        send_dq(i)

    merge((z + 2) % NZ)
    merge(z, part_coef)

    def round_at(i):
        k = i % 4
        ny = (y // 2 + i + i // 4) % 2
        nx = (x + k + (k == 2).astype(jnp.int32) - (k == 3).astype(jnp.int32)) % 4
        return ny * 4 + nx

    def core_rows(i, which):
        return pl.ds(pl.multiple_of(round_at(i) * 4 * T + which * 2 * T, 2 * T), 2 * T)

    def sib_copy(i):
        return remote(
            dkv.at[core_rows(i, 1 - core), :], sib_in.at[i], sib_send.at[i], sib_recv.at[i], sibling, z
        )

    def dkv_copy(i, j):
        row = round_at(i) * 4 + core * 2 + j
        return remote(
            kv_out.at[2 * i + j], kv_in.at[chip], dkv_send.at[2 * i + j], dkv_recv.at[chip], row, z
        )

    def finish(i):
        sib_copy(i).wait_recv()
        for j in range(2):
            rows = pl.ds(pl.multiple_of(round_at(i) * 4 * T + core * 2 * T + j * T, T), T)
            terms = dkv[rows, :] + sib_in[i, pl.ds(j * T, T), :]
            kv_out[2 * i + j, pl.ds(0, T), :] = (terms[:, :D] * SCALE).astype(BF16)
            kv_out[2 * i + j, pl.ds(T, T), :] = terms[:, D:].astype(BF16)
            mine = (i == 0) & (y % 2 == j)

            @pl.when(jnp.logical_not(mine))
            def _():
                dkv_copy(i, j).start()

            @pl.when(mine)
            def _():
                kv_in[chip] = kv_out[2 * i + j]

    def round_step(i):
        c = 2 * round_at(i)

        pair = (z, (z + 2) % NZ)
        left = [chunks_of(s, z, b) - c for b in pair]
        whole = (left[0] > 1) & (left[1] > 1)

        @pl.when(whole)
        def _():
            tile(pair, c, 2)

        def one(j):
            b = (z + 2 * j) % NZ
            rest = chunks_of(s, z, b) - c

            @pl.when((rest > 1) & jnp.logical_not(whole))
            def _():
                tile((b,), c, 2)

            @pl.when(rest == 1)
            def _():
                tile((b,), c, 1)

        each(0, 2, one)
        sib_copy(i).start()

        @pl.when(i > 1)
        def _():
            finish(i - 2)

    each(0, ROUNDS, round_step)
    send_dq(2)
    each(ROUNDS - 2, ROUNDS, finish)

    for i in range(1, NZ):
        o_copy(i).wait_recv()
    out_t[z] = out_t[z] * coef[z] + sum(
        o_in[i - 1].astype(F32) * part_coef[(z - i + NZ) % NZ] for i in range(1, NZ)
    )
    for h in range(HEADS):
        att_rows[:, pl.ds(h * D, D)] = out_t[z, :, pl.ds(h * T, T)].T.astype(BF16)
    att_store = pltpu.make_async_copy(att_rows, att_ref, store_sem.at[0])
    att_store.start()

    each(1, NS // 2, lambda i: k_copy(i).wait_send())
    each(1, NS // 2, lambda i: v_copy(i).wait_send())
    each(0, NS // 2, lambda i: k_pass(i).wait_send())
    each(0, NS // 2, lambda i: v_pass(i).wait_send())

    for i in range(2):
        q_copy(i).wait_send()
        g_copy(i).wait_send()
        q_pass(i).wait_send()
        g_pass(i).wait_send()
    for i in range(1, NZ):
        o_copy(i).wait_send()
    each(0, NZ, lambda b: each(1, NZ, lambda j: st_copy(b, j).wait_send()))


    for i in range(1, NZ):
        dq_copy(i).wait_recv()
    dq_t[z] = (dq_t[z] + sum(dq_in[i].astype(F32) for i in range(NZ - 1))) * SCALE
    for h in range(HEADS):
        gq_rows[:, pl.ds(h * D, D)] = dq_t[z, :, pl.ds(h * T, T)].T.astype(BF16)
    gq_store = pltpu.make_async_copy(gq_rows, gq_ref, store_sem.at[1])
    gq_store.start()

    def drain_kv(i):
        sib_copy(i).wait_send()
        for j in range(2):

            @pl.when((i != 0) | (y % 2 != j))
            def _():
                dkv_copy(i, j).wait_send()

    each(0, ROUNDS, drain_kv)
    for i in range(1, NZ):
        dq_copy(i).wait_send()

    def wait_kv(i):
        row = (i // 2) * 4 + core * 2 + i % 2

        @pl.when(i != chip)
        def _():
            remote(kv_out.at[0], kv_in.at[i], dkv_send.at[0], dkv_recv.at[i], row, z).wait_recv()

    each(0, NS // 2, wait_kv)
    for part in range(4):
        rows = pl.ds(part * T // 4, T // 4)
        gk_rows[rows, :] = jnp.sum(kv_in[:, rows, :].astype(F32), axis=0).astype(BF16)
        rows = pl.ds(T + part * T // 4, T // 4)
        gv_rows[pl.ds(part * T // 4, T // 4), :] = jnp.sum(kv_in[:, rows, :].astype(F32), axis=0).astype(BF16)
    gk_store = pltpu.make_async_copy(gk_rows, gk_ref, store_sem.at[2])
    gv_store = pltpu.make_async_copy(gv_rows, gv_ref, store_sem.at[3])
    gk_store.start()
    gv_store.start()
    att_store.wait()
    gq_store.wait()
    gk_store.wait()
    gv_store.wait()


def hand_on(*refs):
    for i in range(4):
        refs[4 + i][...] = refs[i][...]


def shards(queries, keys, values, grad_out):
    whole = pl.BlockSpec(memory_space=pl.ANY)
    vmem = pl.BlockSpec(memory_space=pltpu.VMEM)
    dma = pltpu.SemaphoreType.DMA
    results = pl.pallas_call(
        kernel,
        out_shape=(
            jax.ShapeDtypeStruct((T, QC), BF16),
            jax.ShapeDtypeStruct((T, QC), BF16),
            jax.ShapeDtypeStruct((T, D), BF16),
            jax.ShapeDtypeStruct((T, D), BF16),
        ),
        in_specs=[whole] * 4,
        out_specs=(whole,) * 4,
        scratch_shapes=[
            pltpu.VMEM((NS, T, D), BF16),
            pltpu.VMEM((NS, T, D), BF16),
            pltpu.VMEM((D, NS * T), BF16),
            pltpu.VMEM((D, NS * T), BF16),
            pltpu.VMEM((NZ, QC, D), BF16),
            pltpu.VMEM((NZ, QC, D), BF16),
            pltpu.VMEM((NZ, D, QC), BF16),
            pltpu.VMEM((NZ, D, QC), BF16),
            pltpu.VMEM((NCH, CK, QC), F32),
            pltpu.VMEM((MAXP, CK, QC), BF16),
            pltpu.VMEM((NZ, D, QC), F32),
            pltpu.VMEM((NZ, D, QC), F32),
            pltpu.VMEM((NZ, NZ, 24, T), F32),
            pltpu.VMEM((NZ, 1, QC), F32),
            pltpu.VMEM((NZ, 1, QC), F32),
            pltpu.VMEM((NZ, 1, QC), F32),
            pltpu.VMEM((NZ, 1, QC), F32),
            pltpu.VMEM((NS * T, 2 * D), F32),
            pltpu.VMEM((ROUNDS, 2 * T, 2 * D), F32),
            pltpu.VMEM((NCH, 2 * T, D), BF16),
            pltpu.VMEM((NS // 2, 2 * T, D), BF16),
            pltpu.VMEM((QC, D), BF16),
            pltpu.VMEM((QC, D), BF16),
            pltpu.VMEM((NZ, D, QC), BF16),
            pltpu.VMEM((NZ - 1, D, QC), BF16),
            pltpu.VMEM((NZ, 1, QC), F32),
            pltpu.VMEM((NZ, D, QC), BF16),
            pltpu.VMEM((NZ - 1, D, QC), BF16),
            dma((NS // 2,)),
            dma((NS,)),
            dma((NS // 2,)),
            dma((NS // 2,)),
            dma((NS,)),
            dma((NS // 2,)),
            dma((2,)),
            dma((NZ,)),
            dma(()),
            dma((2,)),
            dma((2,)),
            dma((NZ,)),
            dma(()),
            dma((2,)),
            dma((NZ, NZ)),
            dma((NZ, NZ)),
            dma((NZ,)),
            dma((NZ - 1,)),
            dma((NZ,)),
            dma((NZ - 1,)),
            dma((ROUNDS,)),
            dma((ROUNDS,)),
            dma((NCH,)),
            dma((NS // 2,)),
            dma((2 + 2 * HEADS,)),
            dma((4,)),
            pltpu.VMEM((T, QC), BF16),
            pltpu.VMEM((T, QC), BF16),
            pltpu.VMEM((T, D), BF16),
            pltpu.VMEM((T, D), BF16),
        ],
        compiler_params=pltpu.CompilerParams(
            collective_id=0, has_side_effects=True, vmem_limit_bytes=60 * 1024 * 1024
        ),
        cost_estimate=pl.CostEstimate(
            flops=10_000_000_000, bytes_accessed=10_000_000, transcendentals=6_500_000
        ),
    )(queries, keys, values, grad_out)
    return pl.pallas_call(
        hand_on,
        out_shape=tuple(jax.ShapeDtypeStruct(r.shape, r.dtype) for r in results),
        in_specs=[vmem] * 4,
        out_specs=(vmem,) * 4,
    )(*results)


def solution(mesh):
    spec = P(("ctxa", "ctxb"), None)
    return jax.shard_map(
        shards,
        mesh=mesh,
        in_specs=(spec,) * 4,
        out_specs=(spec,) * 4,
        check_vma=False,
    )
```
